128 devices in a mesh: dp: 16 (over z, y), fsdp: 8 (over x, core).
Axes of the slice: x: 4, y: 4, z: 4, core: 2. Of those that a mesh axis runs over, the one named last changes fastest.
Arguments:
- inputs: bfloat16 [16, 8, 512, 1536], P('dp', 'fsdp'), may hold values from -40 to 40
- norm_gain: float32 [1536], replicated, may hold values from 0.4 to 1.6
- weight_in: bfloat16 [1536, 3072], P('fsdp'), may hold values from -0.15625 to 0.15625
- kernel: float32 [32, 1536], replicated, may hold values from -2.5 to 2.5
- conv_gain: float32 [1536], replicated, may hold values from 0.4 to 1.6
- weight_out: bfloat16 [1536, 1536], P('fsdp'), may hold values from -0.15625 to 0.15625
- out_grad: bfloat16 [16, 8, 512, 1536], P('dp', 'fsdp'), may hold values from -6 to 6
- pack_dest: int32 [8, 64], P('fsdp'), may hold values from 0 to 63, as said below
- utt_blocks: int32 [8, 32], P('fsdp'), may hold values from 1 to 4, 64 in all within a row
- tail_frames: int32 [8, 32], P('fsdp'), may hold values from 1 to 128
Outputs:
- module_out: bfloat16 [16, 8, 512, 1536], P('dp', 'fsdp')
- input_grad: bfloat16 [16, 8, 512, 1536], P('dp', 'fsdp')
- weight_out_grad: float32 [1536, 1536], P(('dp', 'fsdp'))
- kernel_grad: float32 [32, 1536], replicated
The draws below stay inside these ranges and needn't reach their ends.
Inputs may be any that keep to these rules, and one draw needn't show every extreme that they name: `pack_dest`: each row is a permutation. For every device s the 4 entries s * 4 + k name blocks of 4 different devices (entry // 4), and for each k the entries of the 16 devices name 16 different devices.
All inputs are finite; a program needn't handle non-finite values.
Results may differ from the reference program's by a relative error of at most 0.0069.
Values may be sent and summed in bfloat16 or wider, within the bound.
No kernel may reach another device: no remote copies, remote signals or barrier semaphores. Data moves between devices by JAX's collectives and lax.ppermute only.
A program may use at most 128 MiB of HBM per device.

```python
import math
import jax
import jax.numpy as jnp
import numpy as np
from jax import lax

D = 1536
KERNEL = 32
BLOCK = 128
BLK_DEV = 4
MAXB = 4
ROWS = 512
UTTS = 32
ALL_FRAMES = 65536
N_DP = 16
N_FSDP = 8


def draw_inputs(key, part):
    key_a, key_b, key_c = jax.random.split(jax.random.fold_in(key, 3), 3)
    shape_all = (N_DP, N_FSDP, BLK_DEV * BLOCK, D)
    row_scale = jnp.exp(jax.random.uniform(key_a, (N_DP, N_FSDP, BLK_DEV * BLOCK, 1), minval=math.log(0.3), maxval=math.log(3.0)))
    col_scale = jnp.exp(jax.random.uniform(key_b, (D,), minval=math.log(0.5), maxval=math.log(5.0)))
    base_vals = jax.random.normal(key_c, shape_all)
    return jnp.clip(base_vals * row_scale * col_scale, -40.0, 40.0).astype(jnp.bfloat16)


def draw_kernel(key, part):
    key_a, key_b = jax.random.split(jax.random.fold_in(key, 5), 2)
    col_scale = jnp.exp(jax.random.uniform(key_a, (D,), minval=math.log(0.05), maxval=math.log(0.5)))
    base_vals = jax.random.normal(key_b, (KERNEL, D))
    return jnp.clip(base_vals * col_scale[None, :], -2.5, 2.5)


def draw_pack_dest(key, part):
    row_keys = jax.random.split(jax.random.fold_in(key, 7), N_FSDP)

    def one_row(row_key):
        key_a, key_b, key_c, key_d = jax.random.split(row_key, 4)
        relabel = jax.random.permutation(key_a, N_DP)
        start_pos = jax.random.permutation(key_b, N_DP)
        offsets = jax.random.permutation(key_c, N_DP)[:BLK_DEV]
        slot_keys = jax.random.split(key_d, N_DP)
        slot_order = jax.vmap(lambda slot_key: jax.random.permutation(slot_key, BLK_DEV))(slot_keys)
        source_ids = jnp.arange(N_DP)[:, None]
        within = jnp.arange(BLK_DEV)[None, :]
        target = relabel[(start_pos[source_ids] + offsets[within]) % N_DP]
        slot_pick = slot_order[target, within]
        return (target * BLK_DEV + slot_pick).reshape(-1).astype(jnp.int32)
    return jax.vmap(one_row)(row_keys)


def touch_ends(result, rng, low, top_value):
    shape = result.shape
    place = [jax.random.randint(jax.random.fold_in(rng, axis), (), 0, shape[axis]) for axis in range(len(shape))]
    result = result.at[tuple(place)].set(low)
    longest = shape.index(max(shape))
    place[longest] = (place[longest] + 1) % shape[longest]
    return result.at[tuple(place)].set(top_value)


def strengthened(drawn, key, source, target, blocks, factor):
    owner, partner = [(jnp.arange(drawn.shape[axis_at]) // (drawn.shape[axis_at] // blocks)).reshape([-1 if axis == axis_at else 1 for axis in range(drawn.ndim)]) for axis_at in (source, target)]
    chosen = jax.random.permutation(key, blocks)[partner]
    strong = (owner == chosen) | (owner == (partner + blocks // 2) % blocks)
    return jnp.where(strong, factor * drawn, drawn)


def levels(rng, extent, cuts, low, top_value):
    factor_of = 1.0
    for dim, blocks in cuts:
        heights = jax.random.uniform(jax.random.fold_in(jax.random.fold_in(rng, 6), dim), (blocks,), jnp.float32, low / len(cuts), top_value / len(cuts))
        factor_of = factor_of * jnp.repeat(jnp.exp(heights), extent[dim] // blocks).reshape((-1,) + (1,) * (len(extent) - 1 - dim))
    return factor_of


def split_up(amount, total, reach, skew):
    weights = [(1 << 20) // math.isqrt(rank ** skew) + 1 for rank in range(2, amount + 1)]
    rest, given = total - reach - (amount - 1), [1] * (amount - 1)
    while rest > 0:
        candidates = [i for i in range(amount - 1) if given[i] < reach]
        whole, left = sum([weights[i] for i in candidates]), rest
        for i in candidates:
            extra = min(reach - given[i], max(1, left * weights[i] // whole), rest)
            given[i] = given[i] + extra
            rest = rest - extra
    return np.array([reach] + given)


def ragged(rng, count, total, reach, slope):
    if count == 2:
        one = jax.random.randint(rng, (), max(1, total - reach), min(reach, total - 1) + 1)
        return jnp.stack([one, total - one])
    tallies = jnp.asarray(split_up(count, total, reach, slope), jnp.int32)
    twos = (count - 1) // 2
    giver, sink = tallies[1:1 + 2 * twos:2], tallies[2:2 + 2 * twos:2]
    slack = jnp.minimum(giver - 1, reach - sink)
    passed = jax.random.randint(jax.random.fold_in(rng, 1), (twos,), 0, 1 << 20) % (slack + 1)
    tallies = tallies.at[1:1 + 2 * twos:2].set(giver - passed).at[2:2 + 2 * twos:2].set(sink + passed)
    return tallies[jax.random.permutation(jax.random.fold_in(rng, 2), count)]


def scatter_about(own_key, shape, deviation, most, shards=(), held_as=jnp.bfloat16):
    entries = jax.random.normal(own_key, shape, jnp.float32) * deviation
    if len(shards) > 0:
        entries = levels(own_key, shape, shards, -0.22, 0.18) * entries
    return jnp.clip(entries, min=-most, max=most).astype(held_as)


def gaussian_with(stream_key, shape, spread, limit, cuts, heavy, held_as=jnp.bfloat16):
    result = spread * jax.random.normal(stream_key, shape, jnp.float32)
    if cuts:
        result = result * levels(stream_key, shape, cuts, -0.22, 0.18)
    return jnp.clip(strengthened(result, jax.random.fold_in(stream_key, 3), *heavy), -limit, limit).astype(held_as)


def setup_inputs(seed: int = 0) -> dict:
    seeds = jax.random.split(jax.random.key(seed), 11)
    return {
        "inputs": draw_inputs(jax.random.fold_in(seeds[10], 71), 0),
        "norm_gain": jnp.clip(1.0 + 0.12 * jax.random.normal(seeds[1], (D,), jnp.float32), 0.4, 1.6),
        "weight_in": scatter_about(seeds[2], (D, 2 * D), D ** -0.5, 0.15625, ((0, 8),)),
        "kernel": draw_kernel(jax.random.fold_in(seeds[10], 71), 0),
        "conv_gain": jnp.clip(1.0 + 0.12 * jax.random.normal(seeds[4], (D,), jnp.float32), 0.4, 1.6),
        "weight_out": scatter_about(seeds[5], (D, D), D ** -0.5, 0.15625, ((0, 8),)),
        "out_grad": gaussian_with(seeds[6], (N_DP, N_FSDP, ROWS, D), 1.0, 6.0, ((0, 16), (1, 8)), (0, 3, 16, 2.0)),
        "pack_dest": draw_pack_dest(jax.random.fold_in(seeds[10], 71), 0),
        "utt_blocks": jax.vmap(lambda own: ragged(own, UTTS, N_DP * BLK_DEV, MAXB, 2))(jax.random.split(seeds[8], N_FSDP)).reshape((N_FSDP, UTTS)).astype(jnp.int32),
        "tail_frames": touch_ends(jax.random.randint(seeds[9], (N_FSDP, UTTS), 1, BLOCK + 1), jax.random.fold_in(seeds[9], 1), 1, BLOCK).astype(jnp.int32),
    }


eps = 1e-05

def norm_forward(values, gain_vec):
    average = lax.optimization_barrier(jnp.mean(values, axis=-1, keepdims=True))
    centered = values - average
    inverse = lax.rsqrt(lax.optimization_barrier(jnp.mean(centered * centered, axis=-1, keepdims=True)) + eps)
    normed = centered * inverse
    return (normed * gain_vec, normed, inverse)

def norm_backward(grad_in, normed, inverse):
    first_mean = lax.optimization_barrier(jnp.mean(grad_in, axis=-1, keepdims=True))
    second_mean = lax.optimization_barrier(jnp.mean(grad_in * normed, axis=-1, keepdims=True))
    return (grad_in - first_mean - normed * second_mean) * inverse

def frame_masks(counts, tail_counts, frames, block_len):
    block_ends = jnp.cumsum(counts).astype(jnp.int32)
    block_starts = block_ends - counts
    block_index = frames // block_len
    in_block = frames - block_index * block_len
    inside = (block_index[:, None] >= block_starts[None, :]) & (block_index[:, None] < block_ends[None, :])
    number = jnp.arange(counts.shape[0], dtype=jnp.int32)
    owner_ids = lax.optimization_barrier(jnp.sum(jnp.where(inside, number[None, :] + 1, 0), axis=1)).astype(jnp.int32) - 1
    is_last = block_index[:, None] == block_ends[None, :] - 1
    valid_count = lax.optimization_barrier(jnp.sum(jnp.where(inside, jnp.where(is_last, tail_counts[None, :], block_len), 0), axis=1)).astype(jnp.int32)
    return (owner_ids, in_block < valid_count)

def depthwise(padded, owner_pad, owner_ids, kernel):
    row_count = owner_ids.shape[0]
    running = jnp.zeros((row_count, kernel.shape[1]), jnp.float32)
    for tap_index in range(kernel.shape[0]):
        same_utt = (owner_pad[tap_index:tap_index + row_count] == owner_ids)[:, None]
        running = running + jnp.where(same_utt, padded[tap_index:tap_index + row_count].astype(jnp.float32), 0.0) * kernel[tap_index][None, :]
    return running

def depthwise_transpose(padded, owner_pad, owner_ids, kernel):
    row_count = owner_ids.shape[0]
    tap_count = kernel.shape[0]
    running = jnp.zeros((row_count, kernel.shape[1]), jnp.float32)
    for tap_index in range(tap_count):
        begin = tap_count - tap_index
        same_utt = (owner_pad[begin:begin + row_count] == owner_ids)[:, None]
        running = running + jnp.where(same_utt, padded[begin:begin + row_count].astype(jnp.float32), 0.0) * kernel[tap_index][None, :]
    return running

def kernel_terms(grad_in, padded, owner_pad, owner_ids, tap_count):
    row_count = owner_ids.shape[0]
    grad_wide = grad_in.astype(jnp.float32)
    per_tap = []
    for tap_index in range(tap_count):
        same_utt = (owner_pad[tap_index:tap_index + row_count] == owner_ids)[:, None]
        per_tap.append(lax.optimization_barrier(jnp.sum(jnp.where(same_utt, padded[tap_index:tap_index + row_count].astype(jnp.float32) * grad_wide, 0.0), axis=0)))
    return jnp.stack(per_tap)

def transpose_dot(left, right):
    return lax.dot_general(left, right, (((1,), (1,)), ((), ())), preferred_element_type=jnp.float32)

def reference(inputs, norm_gain, weight_in, kernel, conv_gain, weight_out, out_grad, pack_dest, utt_blocks, tail_frames):
    half_width = KERNEL // 2
    frame_total = N_DP * ROWS
    frame_ids = jnp.arange(frame_total, dtype=jnp.int32)
    pad_ids = jnp.arange(frame_total + 2 * half_width, dtype=jnp.int32) - half_width

    def one_group(running, group_data):
        group_in, group_grad, packing, counts, tail_counts = group_data
        blocks_orig = group_in.reshape(N_DP * BLK_DEV, BLOCK, D)
        packed = jnp.zeros_like(blocks_orig).at[packing].set(blocks_orig).reshape(frame_total, D)
        upstream = group_grad.reshape(frame_total, D)
        owner_ids, valid = frame_masks(counts, tail_counts, frame_ids, BLOCK)
        owner_pad = frame_masks(counts, tail_counts, pad_ids, BLOCK)[0]
        valid_col = valid[:, None]
        scaled_in, normed_in, inverse_in = norm_forward(packed.astype(jnp.float32), norm_gain)
        hidden_in = scaled_in.astype(jnp.bfloat16)
        projected = jnp.dot(hidden_in, weight_in, preferred_element_type=jnp.float32)
        linear_part = projected[:, :D]
        gate_vals = jax.nn.sigmoid(projected[:, D:])
        glu = jnp.where(valid_col, linear_part * gate_vals, 0.0).astype(jnp.bfloat16)
        glu_pad = jnp.pad(glu, ((half_width, half_width), (0, 0)))
        conv = jnp.where(valid_col, depthwise(glu_pad, owner_pad, owner_ids, kernel), 0.0)
        scaled_c, normed_c, inverse_c = norm_forward(conv, conv_gain)
        sigmoid_c = jax.nn.sigmoid(scaled_c)
        swished = (scaled_c * sigmoid_c).astype(jnp.bfloat16)
        module_out = jnp.dot(swished, weight_out, preferred_element_type=jnp.float32).astype(jnp.bfloat16)
        grad_s = transpose_dot(upstream, weight_out)
        weight_term = lax.dot_general(swished, upstream, (((0,), (0,)), ((), ())), preferred_element_type=jnp.float32)
        grad_n = grad_s * sigmoid_c * (1.0 + scaled_c * (1.0 - sigmoid_c))
        grad_conv = jnp.where(valid_col, norm_backward(grad_n * conv_gain, normed_c, inverse_c), 0.0).astype(jnp.bfloat16)
        grad_pad = jnp.pad(grad_conv, ((half_width, half_width), (0, 0)))
        kernel_term = kernel_terms(grad_conv, glu_pad, owner_pad, owner_ids, KERNEL)
        grad_glu = jnp.where(valid_col, depthwise_transpose(grad_pad, owner_pad, owner_ids, kernel), 0.0)
        grad_proj = jnp.concatenate([grad_glu * gate_vals, grad_glu * linear_part * gate_vals * (1.0 - gate_vals)], axis=1).astype(jnp.bfloat16)
        grad_hidden = transpose_dot(grad_proj, weight_in)
        input_grad = norm_backward(grad_hidden * norm_gain, normed_in, inverse_in).astype(jnp.bfloat16)
        carried = (running[0] + weight_term, running[1] + kernel_term)
        return (carried, (module_out.reshape(N_DP, ROWS, D), input_grad.reshape(N_DP, ROWS, D)))
    start_sums = (jnp.zeros((D, D), jnp.float32), jnp.zeros((KERNEL, D), jnp.float32))
    group_inputs = (jnp.swapaxes(inputs, 0, 1), jnp.swapaxes(out_grad, 0, 1), pack_dest, utt_blocks, tail_frames)
    sums, grouped = lax.scan(one_group, start_sums, group_inputs)
    grad_scale = 1.0 / math.sqrt(ALL_FRAMES)
    return (jnp.swapaxes(grouped[0], 0, 1), jnp.swapaxes(grouped[1], 0, 1), sums[0] * grad_scale, sums[1] * grad_scale)
```

```python
import functools
import math

import jax
import jax.numpy as jnp
from jax import lax
from jax.experimental import pallas as pl
from jax.experimental.pallas import tpu as pltpu
from jax.sharding import PartitionSpec as P

BLOCK = 128
LANES = 128
HALF = 16
TAPS = 32
EPS = 1e-05
VMEM = 56 * 2**20
F32 = jnp.float32
BF16 = jnp.bfloat16

LEFT, RIGHT, COUNT, SLOT = 0, 4, 8, 12


def row_mean(values):
    return jnp.mean(values, axis=-1, keepdims=True)


def normalise(values):
    centered = values - row_mean(values)
    inverse = lax.rsqrt(row_mean(centered * centered) + EPS)
    return centered * inverse, inverse


def below(count, rows, first=0):
    return lax.broadcasted_iota(jnp.int32, (rows, 1), 0) + first < count


def params():
    return pltpu.CompilerParams(vmem_limit_bytes=VMEM)


def cost(flops, nbytes, transcendentals=0):
    return pl.CostEstimate(
        flops=flops, bytes_accessed=nbytes, transcendentals=transcendentals
    )


def whole(shape):
    return pl.BlockSpec(shape, lambda *_: (0,) * len(shape))


def reorder_kernel(order, x_ref, o_ref):
    for t in range(x_ref.shape[0]):
        o_ref[t] = x_ref[order[t]]


def reorder(order, x):
    return pl.pallas_call(
        reorder_kernel,
        out_shape=jax.ShapeDtypeStruct(x.shape, x.dtype),
        grid_spec=pltpu.PrefetchScalarGridSpec(
            num_scalar_prefetch=1,
            grid=(1,),
            in_specs=[whole(x.shape)],
            out_specs=whole(x.shape),
        ),
        compiler_params=params(),
        cost_estimate=cost(0, 2 * x.size * 2),
        name="reorder",
    )(order, x)


def project_kernel(
    meta, x_ref, gain_ref, wl_ref, wg_ref, lin_ref, gate_ref, glu_ref, low_ref, high_ref, hidden
):
    blocks = x_ref.shape[0]

    @pl.when(pl.program_id(0) == 0)
    def _():
        for j in range(blocks):
            normed, _ = normalise(x_ref[meta[SLOT + j]].astype(F32))
            hidden[j * BLOCK : (j + 1) * BLOCK] = (normed * gain_ref[...]).astype(BF16)

    held = hidden[...]
    lin = jnp.dot(held, wl_ref[...], preferred_element_type=F32)
    gate = jax.nn.sigmoid(jnp.dot(held, wg_ref[...], preferred_element_type=F32))
    lin_ref[...] = lin
    gate_ref[...] = gate
    for j in range(blocks):
        rows = slice(j * BLOCK, (j + 1) * BLOCK)
        glu = jnp.where(below(meta[COUNT + j], BLOCK), lin[rows] * gate[rows], 0.0).astype(BF16)
        glu_ref[rows] = glu
        if j == 0:
            low_ref[...] = glu[:HALF]
        if j == blocks - 1:
            high_ref[...] = glu[BLOCK - HALF :]


def project(meta, x, gain, weight, tile=256):
    blocks, _, width = x.shape
    rows = blocks * BLOCK
    steps = width // tile
    column = pl.BlockSpec((rows, tile), lambda n, _: (0, n))
    edge = pl.BlockSpec((HALF, tile), lambda n, _: (0, n))
    return pl.pallas_call(
        project_kernel,
        out_shape=[
            jax.ShapeDtypeStruct((rows, width), F32),
            jax.ShapeDtypeStruct((rows, width), F32),
            jax.ShapeDtypeStruct((rows, width), BF16),
            jax.ShapeDtypeStruct((HALF, width), BF16),
            jax.ShapeDtypeStruct((HALF, width), BF16),
        ],
        grid_spec=pltpu.PrefetchScalarGridSpec(
            num_scalar_prefetch=1,
            grid=(steps,),
            in_specs=[
                whole(x.shape),
                whole((1, width)),
                pl.BlockSpec((width, tile), lambda n, _: (0, n)),
                pl.BlockSpec((width, tile), lambda n, _: (0, n + steps)),
            ],
            out_specs=[column, column, column, edge, edge],
            scratch_shapes=[pltpu.VMEM((rows, width), BF16)],
        ),
        compiler_params=params(),
        cost_estimate=cost(4 * rows * width * width, 22 * 2**20),
        name="project",
    )(meta, x, gain, weight, weight)


def fill(pad, left, middle, right, left_ok, right_ok):
    pad[0:HALF] = jnp.where(left_ok > 0, left.astype(F32), 0.0)
    pad[HALF : HALF + BLOCK] = middle.astype(F32)
    pad[HALF + BLOCK :] = jnp.where(right_ok > 0, right.astype(F32), 0.0)


def fill_inner(pad, meta, b, src):
    at = pl.multiple_of(b * BLOCK, BLOCK)
    fill(
        pad,
        src[pl.ds(pl.multiple_of(at - HALF, HALF), HALF)],
        src[pl.ds(at, BLOCK)],
        src[pl.ds(pl.multiple_of(at + BLOCK, BLOCK), HALF)],
        meta[LEFT + b],
        meta[RIGHT + b],
    )


def fill_first(pad, meta, src, low):
    fill(pad, low[...], src[0:BLOCK], src[BLOCK : BLOCK + HALF], meta[LEFT], meta[RIGHT])


def fill_last(pad, meta, src, high):
    rows = src.shape[0]
    last = rows // BLOCK - 1
    fill(
        pad,
        src[rows - BLOCK - HALF : rows - BLOCK],
        src[rows - BLOCK :],
        high[...],
        meta[LEFT + last],
        meta[RIGHT + last],
    )


def slabs(pad, lanes, first):
    for p in range(8):
        offsets = [o for o in range(first, first + TAPS) if o % 8 == p]
        count = BLOCK + 8 * (offsets[-1] // 8)
        yield pad[pl.ds(p, count), lanes].reshape(count // 8, 8, LANES), offsets


def depthwise(pad, taps, lanes, first, tap_of):
    total = jnp.zeros((BLOCK // 8, 8, LANES), F32)
    for slab, offsets in slabs(pad, lanes, first):
        for o in offsets:
            i = tap_of(o)
            total = total + slab[o // 8 : o // 8 + BLOCK // 8] * taps[i : i + 1, lanes][None]
    return total.reshape(BLOCK, LANES)


def lane_tiles(width):
    return lambda body: pl.loop(0, width // LANES)(
        lambda c: body(pl.ds(pl.multiple_of(c * LANES, LANES), LANES))
    )


def pad_by_step(inner, meta, src, low, high, pad):
    step = pl.program_id(0)
    if inner:
        b = step + 1
        fill_inner(pad, meta, b, src)
        return b

    @pl.when(step == 0)
    def _():
        fill_first(pad, meta, src, low)

    @pl.when(step == 1)
    def _():
        fill_last(pad, meta, src, high)

    return step * (src.shape[0] // BLOCK - 1)


def conv_kernel(inner, meta, *refs):
    if inner:
        src, taps, gain, conv_ref, swished_ref, pad = refs
        low = high = None
    else:
        src, taps, gain, low, high, _, _, conv_ref, swished_ref, pad = refs
    b = pad_by_step(inner, meta, src, low, high, pad)
    valid = below(meta[COUNT + b], BLOCK)

    @lane_tiles(src.shape[1])
    def _(lanes):
        conv_ref[:, lanes] = jnp.where(valid, depthwise(pad, taps, lanes, 0, lambda o: o), 0.0)

    @pl.loop(0, BLOCK // 16)
    def _(r):
        rows = pl.ds(pl.multiple_of(r * 16, 16), 16)
        normed, _ = normalise(conv_ref[rows])
        scaled = normed * gain[...]
        swished_ref[rows] = (scaled * jax.nn.sigmoid(scaled)).astype(BF16)


def split_call(kernel, inner, meta, operands, edges, held, outs, width, flops):
    rows = operands[0].shape[0]
    last = rows // BLOCK - 1

    def place(n, _):
        return (n + 1 if inner else n * last, 0)

    in_specs = []
    for a in operands:
        if a.shape[0] == rows and a is not operands[0]:
            in_specs.append(pl.BlockSpec((BLOCK, a.shape[1]), place))
        else:
            in_specs.append(whole(a.shape))
    args = list(operands)
    aliases = {}
    if not inner:
        args += list(edges)
        in_specs += [whole(e.shape) for e in edges]
        for n, h in enumerate(held):
            aliases[1 + len(args)] = n
            args.append(h)
            in_specs.append(pl.BlockSpec(memory_space=pl.ANY))
    return pl.pallas_call(
        functools.partial(kernel, inner),
        out_shape=[jax.ShapeDtypeStruct(*o) for o in outs],
        grid_spec=pltpu.PrefetchScalarGridSpec(
            num_scalar_prefetch=1,
            grid=(2,),
            in_specs=in_specs,
            out_specs=[pl.BlockSpec((BLOCK, o[0][1]), place) for o in outs],
            scratch_shapes=[pltpu.VMEM((BLOCK + 2 * HALF, width), F32)],
        ),
        input_output_aliases=aliases,
        compiler_params=params(),
        cost_estimate=cost(flops, 6 * 2**20),
        name=kernel.__name__ + ("_inner" if inner else "_edges"),
    )(meta, *args)


def conv_forward(inner, meta, glu, taps, gain, edges=(), held=()):
    rows, width = glu.shape
    return split_call(
        conv_kernel,
        inner,
        meta,
        (glu, taps, gain),
        edges,
        held,
        [((rows, width), F32), ((rows, width), BF16)],
        width,
        4 * 10**9,
    )


def grad_conv_kernel(meta, conv_ref, grad_ref, gain_ref, out_ref, low_ref, high_ref):
    b = pl.program_id(0)

    @pl.loop(0, BLOCK // 16)
    def _(r):
        rows = pl.ds(pl.multiple_of(r * 16, 16), 16)
        gain = gain_ref[...]
        normed, inverse = normalise(conv_ref[rows])
        scaled = normed * gain
        sig = jax.nn.sigmoid(scaled)
        g = grad_ref[rows] * sig * (1.0 + scaled * (1.0 - sig)) * gain
        back = (g - row_mean(g) - normed * row_mean(g * normed)) * inverse
        out_ref[rows] = jnp.where(below(meta[COUNT + b], 16, r * 16), back, 0.0).astype(BF16)

    @pl.when(b == 0)
    def _():
        low_ref[...] = out_ref[0:HALF]

    @pl.when(b == pl.num_programs(0) - 1)
    def _():
        high_ref[...] = out_ref[BLOCK - HALF :]


def grad_conv_call(meta, conv, grad_s, gain):
    rows, width = conv.shape
    block = pl.BlockSpec((BLOCK, width), lambda n, _: (n, 0))
    return pl.pallas_call(
        grad_conv_kernel,
        out_shape=[
            jax.ShapeDtypeStruct((rows, width), BF16),
            jax.ShapeDtypeStruct((HALF, width), BF16),
            jax.ShapeDtypeStruct((HALF, width), BF16),
        ],
        grid_spec=pltpu.PrefetchScalarGridSpec(
            num_scalar_prefetch=1,
            grid=(rows // BLOCK,),
            in_specs=[block, block, whole((1, width))],
            out_specs=[block, whole((HALF, width)), whole((HALF, width))],
        ),
        compiler_params=params(),
        cost_estimate=cost(2 * 10**9, 8 * 2**20),
        name="grad_conv",
    )(meta, conv, grad_s, gain)


def taps_kernel(meta, src, grad_ref, low, high, out_ref, pad, total):
    b = pl.program_id(0)
    last = pl.num_programs(0) - 1
    width = src.shape[1]

    @pl.when(b == 0)
    def _():
        fill_first(pad, meta, src, low)
        total[...] = jnp.zeros_like(total)

    @pl.when(b == last)
    def _():
        fill_last(pad, meta, src, high)

    @pl.when((b > 0) & (b < last))
    def _():
        fill_inner(pad, meta, b, src)

    @lane_tiles(width)
    def _(lanes):
        grad = grad_ref[:, lanes].astype(F32).reshape(BLOCK // 8, 8, LANES)
        for slab, offsets in slabs(pad, lanes, 0):
            for o in offsets:
                total[o, :, lanes] += jnp.sum(
                    slab[o // 8 : o // 8 + BLOCK // 8] * grad, axis=0
                )

    @pl.when(b == last)
    def _():
        out_ref[...] = jnp.sum(total[...], axis=1)


def taps_gradient(meta, glu, grad_conv, edges):
    rows, width = glu.shape
    return pl.pallas_call(
        taps_kernel,
        out_shape=jax.ShapeDtypeStruct((TAPS, width), F32),
        grid_spec=pltpu.PrefetchScalarGridSpec(
            num_scalar_prefetch=1,
            grid=(rows // BLOCK,),
            in_specs=[
                whole(glu.shape),
                pl.BlockSpec((BLOCK, width), lambda n, _: (n, 0)),
                whole((HALF, width)),
                whole((HALF, width)),
            ],
            out_specs=whole((TAPS, width)),
            scratch_shapes=[
                pltpu.VMEM((BLOCK + 2 * HALF, width), F32),
                pltpu.VMEM((TAPS, 8, width), F32),
            ],
        ),
        compiler_params=params(),
        cost_estimate=cost(8 * 10**9, 4 * 2**20),
        name="taps_gradient",
    )(meta, glu, grad_conv, *edges)


def back_kernel(inner, meta, *refs):
    if inner:
        src, taps, lin_ref, gate_ref, out_ref, pad = refs
        low = high = None
    else:
        src, taps, lin_ref, gate_ref, low, high, _, out_ref, pad = refs
    width = src.shape[1]
    b = pad_by_step(inner, meta, src, low, high, pad)
    valid = below(meta[COUNT + b], BLOCK)

    @pl.loop(0, width // LANES)
    def _(c):
        at = pl.multiple_of(c * LANES, LANES)
        lanes = pl.ds(at, LANES)
        grad = jnp.where(valid, depthwise(pad, taps, lanes, 1, lambda o: TAPS - o), 0.0)
        gate = gate_ref[:, lanes]
        through = grad * gate
        out_ref[:, lanes] = through.astype(BF16)
        out_ref[:, pl.ds(pl.multiple_of(at + width, LANES), LANES)] = (
            through * lin_ref[:, lanes] * (1.0 - gate)
        ).astype(BF16)


def conv_backward(inner, meta, grad_conv, taps, lin, gate, edges=(), held=()):
    rows, width = grad_conv.shape
    return split_call(
        back_kernel,
        inner,
        meta,
        (grad_conv, taps, lin, gate),
        edges,
        held,
        [((rows, 2 * width), BF16)],
        width,
        4 * 10**9,
    )


def input_kernel(meta, x_ref, gain_ref, grad_ref, w_ref, out_ref, hidden):
    n = pl.program_id(0)
    tile = w_ref.shape[0]
    hidden[:, pl.ds(pl.multiple_of(n * tile, tile), tile)] = lax.dot_general(
        grad_ref[...], w_ref[...], (((1,), (1,)), ((), ())), preferred_element_type=F32
    )

    @pl.when(n == pl.num_programs(0) - 1)
    def _():
        for j in range(x_ref.shape[0]):
            rows = slice(j * BLOCK, (j + 1) * BLOCK)
            normed, inverse = normalise(x_ref[meta[SLOT + j]].astype(F32))
            g = hidden[rows] * gain_ref[...]
            out_ref[rows] = (
                (g - row_mean(g) - normed * row_mean(g * normed)) * inverse
            ).astype(BF16)


def input_gradient(meta, x, gain, grad_proj, weight, tile=256):
    rows = grad_proj.shape[0]
    width = weight.shape[0]
    return pl.pallas_call(
        input_kernel,
        out_shape=jax.ShapeDtypeStruct((rows, width), BF16),
        grid_spec=pltpu.PrefetchScalarGridSpec(
            num_scalar_prefetch=1,
            grid=(width // tile,),
            in_specs=[
                whole(x.shape),
                whole((1, width)),
                whole(grad_proj.shape),
                pl.BlockSpec((tile, weight.shape[1]), lambda n, _: (n, 0)),
            ],
            out_specs=whole((rows, width)),
            scratch_shapes=[pltpu.VMEM((rows, width), F32)],
        ),
        compiler_params=params(),
        cost_estimate=cost(4 * rows * width * width, 16 * 2**20),
        name="input_gradient",
    )(meta, x, gain, grad_proj, weight)


def halves_of_neighbours(low, high):
    count = lax.axis_size("dp")
    forward = [(i, i + 1) for i in range(count - 1)]
    backward = [(i + 1, i) for i in range(count - 1)]
    return lax.ppermute(high, "dp", forward), lax.ppermute(low, "dp", backward)


def swap(values, axis, bits):
    return lax.ppermute(values, axis, [(i, i ^ bits) for i in range(lax.axis_size(axis))])


def sum_of_four(values, axis, low_bit):
    one, two = low_bit, 2 * low_bit
    first, second, third = (swap(values, axis, b) for b in (one, two, one + two))
    return (values + first) + (second + third)


def sum_everywhere(values, core):
    half = values.shape[0] // 2
    own = lax.dynamic_slice_in_dim(values, core * half, half)
    other = lax.dynamic_slice_in_dim(values, (1 - core) * half, half)
    own = own + swap(other, "fsdp", 1)
    own = sum_of_four(own, "fsdp", 2)
    own = sum_of_four(own, "dp", 1)
    own = sum_of_four(own, "dp", 4)
    other = swap(own, "fsdp", 1)
    return jnp.where(
        core == 0, jnp.concatenate([own, other]), jnp.concatenate([other, own])
    )


def spread(values, axis):
    return lax.all_to_all(values, axis, split_axis=0, concat_axis=0, tiled=True)


def outer(left, right):
    return lax.dot_general(left, right, (((0,), (0,)), ((), ())), preferred_element_type=F32)


def summed_outer(left, right, core, scale):
    width = right.shape[1]
    half = width // 2
    dp_count, fsdp_count = lax.axis_size("dp"), lax.axis_size("fsdp")
    ours = lax.dynamic_slice_in_dim(right, core * half, half, axis=1)
    theirs = lax.dynamic_slice_in_dim(right, (1 - core) * half, half, axis=1)
    arrived = swap(outer(left, theirs).astype(BF16), "fsdp", 1)
    both = (outer(left, ours) + arrived.astype(F32)).astype(BF16)
    rows = left.shape[1] // dp_count
    over_dp = jnp.sum(spread(both.reshape(dp_count, rows, half), "dp").astype(F32), axis=0)
    rows //= fsdp_count
    pieces = spread((over_dp * scale).reshape(fsdp_count, rows, half), "fsdp")
    pieces = jnp.sum(pieces.reshape(fsdp_count // 2, 2, rows, half), axis=0)
    return jnp.concatenate([pieces[0], pieces[1]], axis=1)


def scalars(packing, counts, tails, place, blocks):
    mine = place * blocks + jnp.arange(blocks, dtype=jnp.int32)
    number = jnp.arange(counts.shape[0], dtype=jnp.int32)
    ends = jnp.sum(jnp.where(number[:, None] <= number[None, :], counts[:, None], 0), axis=0)
    opens = (ends - counts)[None, :] == mine[:, None]
    closes = (ends - 1)[None, :] == mine[:, None]
    left = 1 - jnp.sum(opens.astype(jnp.int32), axis=1)
    right = 1 - jnp.sum(closes.astype(jnp.int32), axis=1)
    valid = BLOCK + jnp.sum(jnp.where(closes, tails[None, :] - BLOCK, 0), axis=1)
    number = jnp.arange(packing.shape[0], dtype=jnp.int32)
    slot = jnp.sum(
        jnp.where(packing[None, :] == mine[:, None], number[None, :] % blocks, 0), axis=1
    )
    return jnp.concatenate([left, right, valid, slot]).astype(jnp.int32)


def target_order(packing, place, blocks):
    count = packing.shape[0] // blocks
    color = place // blocks
    number = jnp.arange(packing.shape[0], dtype=jnp.int32)
    chosen = (number % blocks == color)[None, :]
    goes = (packing // blocks)[None, :] == jnp.arange(count, dtype=jnp.int32)[:, None]
    return jnp.sum(jnp.where(chosen & goes, (number // blocks)[None, :], 0), axis=1)


def local(
    inputs,
    norm_gain,
    weight_in,
    kernel,
    conv_gain,
    weight_out,
    out_grad,
    pack_dest,
    utt_blocks,
    tail_frames,
):
    dp_count = lax.axis_size("dp")
    place = lax.axis_index("dp")
    core = lax.axis_index("fsdp") % 2
    rows, width = inputs.shape[2:]
    blocks = rows // BLOCK
    scale = 1.0 / math.sqrt(rows * lax.axis_size(("dp", "fsdp")))
    full_in = lax.all_gather(weight_in, "fsdp", axis=0, tiled=True)
    full_out = lax.all_gather(weight_out, "fsdp", axis=0, tiled=True)
    meta = scalars(pack_dest[0], utt_blocks[0], tail_frames[0], place, blocks)
    order = target_order(pack_dest[0], place, blocks)
    gain_in = norm_gain.reshape(1, width)
    gain_conv = conv_gain.reshape(1, width)

    quarters = spread(inputs.reshape(dp_count, rows // dp_count, width), "dp")
    arrived = spread(reorder(order, quarters), "dp").reshape(blocks, BLOCK, width)

    lin, gate, glu, low, high = project(meta, arrived, gain_in, full_in)
    glu_edges = halves_of_neighbours(low, high)
    held = conv_forward(True, meta, glu, kernel, gain_conv)
    conv, swished = conv_forward(False, meta, glu, kernel, gain_conv, glu_edges, held)

    upstream = out_grad[0, 0]
    weight_out_grad = summed_outer(swished, upstream, core, scale)
    grad_s = lax.dot_general(
        upstream, full_out, (((1,), (1,)), ((), ())), preferred_element_type=F32
    )
    grad_conv, low, high = grad_conv_call(meta, conv, grad_s, gain_conv)
    edges = halves_of_neighbours(low, high)
    taps_grad = taps_gradient(meta, glu, grad_conv, glu_edges)
    kernel_grad = sum_everywhere(taps_grad * scale, core)
    held = conv_backward(True, meta, grad_conv, kernel, lin, gate)
    [grad_proj] = conv_backward(False, meta, grad_conv, kernel, lin, gate, edges, held)
    input_grad = input_gradient(meta, arrived, gain_in, grad_proj, full_in)
    module_out = jnp.dot(swished, full_out, preferred_element_type=F32).astype(BF16)
    return (
        module_out.reshape(1, 1, rows, width),
        input_grad.reshape(1, 1, rows, width),
        weight_out_grad,
        kernel_grad,
    )


def solution(mesh):
    in_specs = (
        P("dp", "fsdp", None, None),
        P(),
        P("fsdp", None),
        P(),
        P(),
        P("fsdp", None),
        P("dp", "fsdp", None, None),
        P("fsdp", None),
        P("fsdp", None),
        P("fsdp", None),
    )
    out_specs = (
        P("dp", "fsdp", None, None),
        P("dp", "fsdp", None, None),
        P(("dp", "fsdp"), None),
        P(),
    )
    return jax.shard_map(local, mesh=mesh, in_specs=in_specs, out_specs=out_specs, check_vma=False)
```

```python
import functools
import math

import jax
import jax.numpy as jnp
from jax import lax
from jax.experimental import pallas as pl
from jax.experimental.pallas import tpu as pltpu
from jax.sharding import PartitionSpec as P

BLOCK = 128
LANES = 128
HALF = 16
TAPS = 32
EPS = 1e-05
VMEM = 28 * 2**20
F32 = jnp.float32
BF16 = jnp.bfloat16

LEFT, RIGHT, COUNT, SLOT = 0, 4, 8, 12


def row_mean(values):
    return jnp.mean(values, axis=-1, keepdims=True)


def normalise(values):
    centered = values - row_mean(values)
    inverse = lax.rsqrt(row_mean(centered * centered) + EPS)
    return centered * inverse, inverse


def below(count, rows, first=0):
    return lax.broadcasted_iota(jnp.int32, (rows, 1), 0) + first < count


def in_hbm(x):
    return pltpu.with_memory_space_constraint(x, pltpu.HBM)


def in_vmem(x):
    return pltpu.with_memory_space_constraint(x, pltpu.VMEM)


def params():
    return pltpu.CompilerParams(vmem_limit_bytes=VMEM)


def cost():
    return pl.CostEstimate(flops=1000, bytes_accessed=1000, transcendentals=0)


def whole(shape):
    return pl.BlockSpec(shape, lambda *_: (0,) * len(shape))


def reorder_kernel(order, x_ref, o_ref):
    for t in range(x_ref.shape[0]):
        o_ref[t] = x_ref[order[t]]


def reorder(order, x):
    return pl.pallas_call(
        reorder_kernel,
        out_shape=pltpu.HBM(x.shape, x.dtype),
        grid_spec=pltpu.PrefetchScalarGridSpec(
            num_scalar_prefetch=1,
            grid=(1,),
            in_specs=[whole(x.shape)],
            out_specs=whole(x.shape),
        ),
        compiler_params=params(),
        cost_estimate=cost(),
        name="reorder",
    )(order, in_vmem(x))


def tiles(width):
    return [slice(at, at + LANES) for at in range(0, width, LANES)]


def row_total(parts):
    return jnp.sum(functools.reduce(lambda a, b: a + b, parts), axis=1, keepdims=True)


def row_stats(load, width):
    mean = row_total(load(t) for t in tiles(width)) * (1.0 / width)

    def squared(t):
        centered = load(t) - mean
        return centered * centered

    var = row_total(squared(t) for t in tiles(width)) * (1.0 / width)
    return mean, lax.rsqrt(var + EPS)


def project_kernel(
    meta, x_ref, gain_ref, wl_ref, wg_ref,
    normed_ref, inverse_ref, gate_ref, slope_ref, glu_ref, low_ref, high_ref, hidden,
):
    count, quarter, width = x_ref.shape
    blocks = count * quarter // BLOCK
    quarters = count // blocks

    @pl.when(pl.program_id(0) == 0)
    def _():
        for j in range(blocks):
            rows = slice(j * BLOCK, (j + 1) * BLOCK)
            first = meta[SLOT + j] * quarters

            def load(t, first=first):
                return jnp.concatenate([x_ref[first + q, :, t] for q in range(quarters)]).astype(F32)

            mean, inverse = row_stats(load, width)
            inverse_ref[rows] = inverse
            for t in tiles(width):
                normed = (load(t) - mean) * inverse
                normed_ref[rows, t] = normed.astype(BF16)
                hidden[rows, t] = (normed * gain_ref[:, t]).astype(BF16)

    held = hidden[...]
    lin = jnp.dot(held, wl_ref[...], preferred_element_type=F32)
    gate = jax.nn.sigmoid(jnp.dot(held, wg_ref[...], preferred_element_type=F32))
    product = lin * gate
    gate_ref[...] = gate
    slope_ref[...] = product * (1.0 - gate)
    for j in range(blocks):
        rows = slice(j * BLOCK, (j + 1) * BLOCK)
        glu = jnp.where(below(meta[COUNT + j], BLOCK), product[rows], 0.0).astype(BF16)
        glu_ref[rows] = glu
        if j == 0:
            low_ref[...] = glu[:HALF]
        if j == blocks - 1:
            high_ref[...] = glu[BLOCK - HALF :]


def project(meta, x, gain, weight, tile=512):
    count, quarter, width = x.shape
    rows = count * quarter
    steps = width // tile
    column = pl.BlockSpec((rows, tile), lambda n, _: (0, n))
    edge = pl.BlockSpec((HALF, tile), lambda n, _: (0, n))
    return pl.pallas_call(
        project_kernel,
        out_shape=[
            pltpu.HBM((rows, width), BF16),
            jax.ShapeDtypeStruct((rows, 1), F32),
            pltpu.HBM((rows, width), F32),
            pltpu.HBM((rows, width), F32),
            jax.ShapeDtypeStruct((rows, width), BF16),
            jax.ShapeDtypeStruct((HALF, width), BF16),
            jax.ShapeDtypeStruct((HALF, width), BF16),
        ],
        grid_spec=pltpu.PrefetchScalarGridSpec(
            num_scalar_prefetch=1,
            grid=(steps,),
            in_specs=[
                whole(x.shape),
                whole((1, width)),
                pl.BlockSpec((width, tile), lambda n, _: (0, n)),
                pl.BlockSpec((width, tile), lambda n, _: (0, n + steps)),
            ],
            out_specs=[whole((rows, width)), whole((rows, 1)), column, column, column, edge, edge],
            scratch_shapes=[pltpu.VMEM((rows, width), BF16)],
        ),
        compiler_params=params(),
        cost_estimate=cost(),
        name="project",
    )(meta, in_hbm(x), gain, in_hbm(weight), in_hbm(weight))


def fill(pad, left, middle, right, left_ok, right_ok):
    pad[0:HALF] = jnp.where(left_ok > 0, left.astype(F32), 0.0)
    pad[HALF : HALF + BLOCK] = middle.astype(F32)
    pad[HALF + BLOCK :] = jnp.where(right_ok > 0, right.astype(F32), 0.0)


def fill_inner(pad, meta, b, src):
    at = pl.multiple_of(b * BLOCK, BLOCK)
    fill(
        pad,
        src[pl.ds(pl.multiple_of(at - HALF, HALF), HALF)],
        src[pl.ds(at, BLOCK)],
        src[pl.ds(pl.multiple_of(at + BLOCK, BLOCK), HALF)],
        meta[LEFT + b],
        meta[RIGHT + b],
    )


def fill_first(pad, meta, src, low):
    fill(pad, low[...], src[0:BLOCK], src[BLOCK : BLOCK + HALF], meta[LEFT], meta[RIGHT])


def fill_last(pad, meta, src, high):
    rows = src.shape[0]
    last = rows // BLOCK - 1
    fill(
        pad,
        src[rows - BLOCK - HALF : rows - BLOCK],
        src[rows - BLOCK :],
        high[...],
        meta[LEFT + last],
        meta[RIGHT + last],
    )


def slabs(pad, lanes, first):
    for p in range(8):
        offsets = [o for o in range(first, first + TAPS) if o % 8 == p]
        count = BLOCK + 8 * (offsets[-1] // 8)
        yield pad[pl.ds(p, count), lanes].reshape(count // 8, 8, LANES), offsets


def depthwise(pad, taps, lanes, first, tap_of):
    total = jnp.zeros((BLOCK // 8, 8, LANES), F32)
    for slab, offsets in slabs(pad, lanes, first):
        for o in offsets:
            i = tap_of(o)
            total = total + slab[o // 8 : o // 8 + BLOCK // 8] * taps[i : i + 1, lanes][None]
    return total.reshape(BLOCK, LANES)


def lane_tiles(width):
    return lambda body: pl.loop(0, width // LANES)(
        lambda c: body(pl.ds(pl.multiple_of(c * LANES, LANES), LANES))
    )


def pad_by_step(inner, meta, src, low, high, pad):
    step = pl.program_id(0)
    if inner:
        b = step + 1
        fill_inner(pad, meta, b, src)
        return b

    @pl.when(step == 0)
    def _():
        fill_first(pad, meta, src, low)

    @pl.when(step == 1)
    def _():
        fill_last(pad, meta, src, high)

    return step * (src.shape[0] // BLOCK - 1)


def conv_kernel(inner, meta, *refs):
    if inner:
        src, taps, gain, normed_ref, inverse_ref, slope_ref, swished_ref, pad, conv = refs
        low = high = None
    else:
        src, taps, gain, low, high, _, _, _, _, *refs = refs
        normed_ref, inverse_ref, slope_ref, swished_ref, pad, conv = refs
    width = src.shape[1]
    b = pad_by_step(inner, meta, src, low, high, pad)
    valid = below(meta[COUNT + b], BLOCK)

    @lane_tiles(width)
    def _(lanes):
        conv[:, lanes] = jnp.where(valid, depthwise(pad, taps, lanes, 0, lambda o: o), 0.0)

    mean, inverse = row_stats(lambda t: conv[:, t], width)
    inverse_ref[...] = inverse
    for t in tiles(width):
        normed = (conv[:, t] - mean) * inverse
        scaled = normed * gain[:, t]
        sig = jax.nn.sigmoid(scaled)
        swished = scaled * sig
        normed_ref[:, t] = normed.astype(BF16)
        swished_ref[:, t] = swished.astype(BF16)
        slope_ref[:, t] = (sig + swished * (1.0 - sig)) * gain[:, t]


def split_call(kernel, inner, meta, operands, edges, held, outs, width, flops):
    rows = operands[0].shape[0]
    last = rows // BLOCK - 1

    def place(n, _):
        return (n + 1 if inner else n * last, 0)

    in_specs = []
    for a in operands:
        if a.shape[0] == rows and a is not operands[0]:
            in_specs.append(pl.BlockSpec((BLOCK, a.shape[1]), place))
        else:
            in_specs.append(whole(a.shape))
    args = list(operands)
    aliases = {}
    if not inner:
        args += list(edges)
        in_specs += [whole(e.shape) for e in edges]
        for n, h in enumerate(held):
            aliases[1 + len(args)] = n
            args.append(h)
            in_specs.append(pl.BlockSpec(memory_space=pl.ANY))
    return pl.pallas_call(
        functools.partial(kernel, inner),
        out_shape=[jax.ShapeDtypeStruct(*o) for o in outs],
        grid_spec=pltpu.PrefetchScalarGridSpec(
            num_scalar_prefetch=1,
            grid=(2,),
            in_specs=in_specs,
            out_specs=[pl.BlockSpec((BLOCK, o[0][1]), place) for o in outs],
            scratch_shapes=[
                pltpu.VMEM((BLOCK + 2 * HALF, width), F32),
                pltpu.VMEM((BLOCK, width), F32),
            ],
        ),
        input_output_aliases=aliases,
        compiler_params=params(),
        cost_estimate=cost(),
        name=kernel.__name__ + ("_inner" if inner else "_edges"),
    )(meta, *args)


def conv_forward(inner, meta, glu, taps, gain, edges=(), held=()):
    rows, width = glu.shape
    return split_call(
        conv_kernel,
        inner,
        meta,
        (glu, taps, gain),
        edges,
        held,
        [((rows, width), BF16), ((rows, 1), F32), ((rows, width), F32), ((rows, width), BF16)],
        width,
        4 * 10**9,
    )


def multiply_kernel(x_ref, w_ref, out_ref):
    out_ref[...] = jnp.dot(x_ref[...], w_ref[...], preferred_element_type=F32).astype(BF16)


def multiply(x, weight, tile=512):
    rows, depth = x.shape
    width = weight.shape[1]
    return pl.pallas_call(
        multiply_kernel,
        out_shape=jax.ShapeDtypeStruct((rows, width), BF16),
        grid=(width // tile,),
        in_specs=[whole((rows, depth)), pl.BlockSpec((depth, tile), lambda n: (0, n))],
        out_specs=pl.BlockSpec((rows, tile), lambda n: (0, n)),
        compiler_params=params(),
        cost_estimate=cost(),
        name="multiply",
    )(x, in_hbm(weight))


def norm_back(load, normed_ref, inverse_ref, rows, width):
    normed = {t.start: normed_ref[rows, t].astype(F32) for t in tiles(width)}
    first = row_total(load(t) for t in tiles(width)) * (1.0 / width)
    second = row_total(load(t) * normed[t.start] for t in tiles(width)) * (1.0 / width)
    inverse = inverse_ref[rows]
    for t in tiles(width):
        yield t, (load(t) - first - normed[t.start] * second) * inverse


def grad_conv_kernel(
    meta, normed_ref, inverse_ref, slope_ref, grad_ref, out_ref, low_ref, high_ref
):
    b = pl.program_id(0)
    valid = below(meta[COUNT + b], BLOCK)
    for t, back in norm_back(
        lambda t: grad_ref[:, t] * slope_ref[:, t],
        normed_ref,
        inverse_ref,
        slice(None),
        normed_ref.shape[1],
    ):
        out_ref[:, t] = jnp.where(valid, back, 0.0).astype(BF16)

    @pl.when(b == 0)
    def _():
        low_ref[...] = out_ref[0:HALF]

    @pl.when(b == pl.num_programs(0) - 1)
    def _():
        high_ref[...] = out_ref[BLOCK - HALF :]


def grad_conv_call(meta, normed, inverse, slope, grad_s):
    rows, width = normed.shape
    block = pl.BlockSpec((BLOCK, width), lambda n, _: (n, 0))
    return pl.pallas_call(
        grad_conv_kernel,
        out_shape=[
            jax.ShapeDtypeStruct((rows, width), BF16),
            jax.ShapeDtypeStruct((HALF, width), BF16),
            jax.ShapeDtypeStruct((HALF, width), BF16),
        ],
        grid_spec=pltpu.PrefetchScalarGridSpec(
            num_scalar_prefetch=1,
            grid=(rows // BLOCK,),
            in_specs=[block, pl.BlockSpec((BLOCK, 1), lambda n, _: (n, 0)), block, block],
            out_specs=[block, whole((HALF, width)), whole((HALF, width))],
        ),
        compiler_params=params(),
        cost_estimate=cost(),
        name="grad_conv",
    )(meta, normed, inverse, slope, grad_s)


def pad_by_block(meta, src, low, high, pad):
    b = pl.program_id(0)
    last = pl.num_programs(0) - 1

    @pl.when(b == 0)
    def _():
        fill_first(pad, meta, src, low)

    @pl.when(b == last)
    def _():
        fill_last(pad, meta, src, high)

    @pl.when((b > 0) & (b < last))
    def _():
        fill_inner(pad, meta, b, src)


def taps_kernel(scale, meta, src, grad_ref, low, high, out_ref, pad, total):
    b = pl.program_id(0)
    last = pl.num_programs(0) - 1
    width = src.shape[1]
    pad_by_block(meta, src, low, high, pad)

    @pl.when(b == 0)
    def _():
        total[...] = jnp.zeros_like(total)

    @lane_tiles(width)
    def _(lanes):
        grad = grad_ref[:, lanes].astype(F32).reshape(BLOCK // 8, 8, LANES)
        for slab, offsets in slabs(pad, lanes, 0):
            for o in offsets:
                total[o, :, lanes] += jnp.sum(
                    slab[o // 8 : o // 8 + BLOCK // 8] * grad, axis=0
                )

    @pl.when(b == last)
    def _():
        groups, few = out_ref.shape[0], out_ref.shape[1] // 2
        half = width // 2
        for g in range(groups):
            own = jnp.sum(total[g * few : (g + 1) * few], axis=1) * scale
            out_ref[g, :few] = own[:, :half]
            out_ref[g, few:] = own[:, half:]


def taps_gradient(meta, glu, grad_conv, edges, groups, scale):
    rows, width = glu.shape
    return pl.pallas_call(
        functools.partial(taps_kernel, scale),
        out_shape=jax.ShapeDtypeStruct((groups, 2 * TAPS // groups, width // 2), F32),
        grid_spec=pltpu.PrefetchScalarGridSpec(
            num_scalar_prefetch=1,
            grid=(rows // BLOCK,),
            in_specs=[
                whole(glu.shape),
                pl.BlockSpec((BLOCK, width), lambda n, _: (n, 0)),
                whole((HALF, width)),
                whole((HALF, width)),
            ],
            out_specs=whole((groups, 2 * TAPS // groups, width // 2)),
            scratch_shapes=[
                pltpu.VMEM((BLOCK + 2 * HALF, width), F32),
                pltpu.VMEM((TAPS, 8, width), F32),
            ],
        ),
        compiler_params=params(),
        cost_estimate=cost(),
        name="taps_gradient",
    )(meta, glu, grad_conv, *edges)


def back_kernel(meta, src, taps, gate_ref, slope_ref, low, high, out_ref, pad):
    b = pl.program_id(0)
    width = src.shape[1]
    pad_by_block(meta, src, low, high, pad)
    valid = below(meta[COUNT + b], BLOCK)

    @pl.loop(0, width // LANES)
    def _(c):
        at = pl.multiple_of(c * LANES, LANES)
        lanes = pl.ds(at, LANES)
        grad = jnp.where(valid, depthwise(pad, taps, lanes, 1, lambda o: TAPS - o), 0.0)
        out_ref[:, lanes] = (grad * gate_ref[:, lanes]).astype(BF16)
        out_ref[:, pl.ds(pl.multiple_of(at + width, LANES), LANES)] = (
            grad * slope_ref[:, lanes]
        ).astype(BF16)


def conv_backward(meta, grad_conv, taps, gate, slope, edges):
    rows, width = grad_conv.shape
    block = pl.BlockSpec((BLOCK, width), lambda n, _: (n, 0))
    return pl.pallas_call(
        back_kernel,
        out_shape=pltpu.HBM((rows, 2 * width), BF16),
        grid_spec=pltpu.PrefetchScalarGridSpec(
            num_scalar_prefetch=1,
            grid=(rows // BLOCK,),
            in_specs=[
                whole(grad_conv.shape),
                whole(taps.shape),
                block,
                block,
                whole((HALF, width)),
                whole((HALF, width)),
            ],
            out_specs=pl.BlockSpec((BLOCK, 2 * width), lambda n, _: (n, 0)),
            scratch_shapes=[pltpu.VMEM((BLOCK + 2 * HALF, width), F32)],
        ),
        compiler_params=params(),
        cost_estimate=cost(),
        name="conv_backward",
    )(meta, grad_conv, taps, in_hbm(gate), in_hbm(slope), *edges)


def input_kernel(gain_ref, grad_ref, w_ref, normed_ref, inverse_ref, out_ref, hidden):
    n = pl.program_id(0)
    rows, width = hidden.shape
    tile = w_ref.shape[0]
    at = pl.ds(pl.multiple_of(n * tile, tile), tile)
    hidden[:, at] = gain_ref[:, at] * lax.dot_general(
        grad_ref[...], w_ref[...], (((1,), (1,)), ((), ())), preferred_element_type=F32
    )

    @pl.when(n == pl.num_programs(0) - 1)
    def _():
        for at in range(0, rows, BLOCK):
            part = slice(at, at + BLOCK)
            for t, back in norm_back(
                lambda t, part=part: hidden[part, t], normed_ref, inverse_ref, part, width
            ):
                out_ref[part, t] = back.astype(BF16)


def input_gradient(gain, grad_proj, weight, normed, inverse, tile=512):
    rows = grad_proj.shape[0]
    width = weight.shape[0]
    return pl.pallas_call(
        input_kernel,
        out_shape=jax.ShapeDtypeStruct((rows, width), BF16),
        grid=(width // tile,),
        in_specs=[
            whole((1, width)),
            whole(grad_proj.shape),
            pl.BlockSpec((tile, weight.shape[1]), lambda n: (n, 0)),
            whole(normed.shape),
            whole(inverse.shape),
        ],
        out_specs=whole((rows, width)),
        scratch_shapes=[pltpu.VMEM((rows, width), F32)],
        compiler_params=params(),
        cost_estimate=cost(),
        name="input_gradient",
    )(gain, in_hbm(grad_proj), in_hbm(weight), in_hbm(normed), inverse)


def halves_of_neighbours(low, high):
    count = lax.axis_size("dp")
    forward = [(i, i + 1) for i in range(count - 1)]
    backward = [(i + 1, i) for i in range(count - 1)]
    return lax.ppermute(high, "dp", forward), lax.ppermute(low, "dp", backward)


def swap(values, axis, bits):
    return lax.ppermute(values, axis, [(i, i ^ bits) for i in range(lax.axis_size(axis))])


def sum_of_four(values, axis, low_bit):
    one, two = low_bit, 2 * low_bit
    first, second, third = (swap(values, axis, b) for b in (one, two, one + two))
    return (values + first) + (second + third)


def sum_of_chip(groups, core):
    groups = groups.reshape((groups.shape[0] // 2, 2) + groups.shape[1:])
    other = lax.dynamic_index_in_dim(groups, 1 - core, axis=1, keepdims=False)
    own = lax.dynamic_index_in_dim(groups, core, axis=1, keepdims=False)
    return own + swap(other, "fsdp", 1)


def sum_along_x(groups):
    mine = lax.axis_index("fsdp") // 2
    total = lax.dynamic_index_in_dim(groups, mine, keepdims=False)
    for bits in range(1, groups.shape[0]):
        theirs = lax.dynamic_index_in_dim(groups, mine ^ bits, keepdims=False)
        total = total + swap(theirs, "fsdp", 2 * bits)
    return total


def spread(values, axis):
    return lax.all_to_all(values, axis, split_axis=0, concat_axis=0, tiled=True)


def outer(left, right):
    return lax.dot_general(left, right, (((0,), (0,)), ((), ())), preferred_element_type=F32)


def outer_of_chip(left, right, core):
    half = right.shape[1] // 2
    ours = lax.dynamic_slice_in_dim(right, core * half, half, axis=1)
    theirs = lax.dynamic_slice_in_dim(right, (1 - core) * half, half, axis=1)
    arrived = swap(outer(left, theirs).astype(BF16), "fsdp", 1)
    return (outer(left, ours) + arrived.astype(F32)).astype(BF16)


def send_over_dp(both):
    count = lax.axis_size("dp")
    return spread(both.reshape((count, both.shape[0] // count) + both.shape[1:]), "dp")


def summed_over_dp(sent, scale):
    total = jnp.sum(sent.astype(F32), axis=0) * scale
    count = lax.axis_size("fsdp")
    return total.reshape((count, total.shape[0] // count) + total.shape[1:])


def last_exchange(taps_rows, pieces):
    taps_rows = jnp.broadcast_to(taps_rows[None], pieces.shape[:1] + taps_rows.shape)
    return spread(jnp.concatenate([taps_rows, pieces], axis=1), "fsdp")


def after_exchange(got, few):
    count, _, half = got.shape
    left = got[:, :few].reshape(count * few, half)
    right = got[:, few : 2 * few].reshape(count * few, half)
    pieces = got[:, 2 * few :]
    pieces = jnp.sum(pieces.reshape((count // 2, 2) + pieces.shape[1:]), axis=0)
    return (
        jnp.concatenate([left, right], axis=1),
        jnp.concatenate([pieces[0], pieces[1]], axis=1),
    )


def scalars(packing, counts, tails, place, blocks):
    mine = place * blocks + jnp.arange(blocks, dtype=jnp.int32)
    number = jnp.arange(counts.shape[0], dtype=jnp.int32)
    ends = jnp.sum(jnp.where(number[:, None] <= number[None, :], counts[:, None], 0), axis=0)
    opens = (ends - counts)[None, :] == mine[:, None]
    closes = (ends - 1)[None, :] == mine[:, None]
    left = 1 - jnp.sum(opens.astype(jnp.int32), axis=1)
    right = 1 - jnp.sum(closes.astype(jnp.int32), axis=1)
    valid = BLOCK + jnp.sum(jnp.where(closes, tails[None, :] - BLOCK, 0), axis=1)
    number = jnp.arange(packing.shape[0], dtype=jnp.int32)
    slot = jnp.sum(
        jnp.where(packing[None, :] == mine[:, None], number[None, :] % blocks, 0), axis=1
    )
    return jnp.concatenate([left, right, valid, slot]).astype(jnp.int32)


def target_order(packing, place, blocks):
    count = packing.shape[0] // blocks
    color = place // blocks
    number = jnp.arange(packing.shape[0], dtype=jnp.int32)
    chosen = (number % blocks == color)[None, :]
    goes = (packing // blocks)[None, :] == jnp.arange(count, dtype=jnp.int32)[:, None]
    return jnp.sum(jnp.where(chosen & goes, (number // blocks)[None, :], 0), axis=1)


def local(
    inputs,
    norm_gain,
    weight_in,
    kernel,
    conv_gain,
    weight_out,
    out_grad,
    pack_dest,
    utt_blocks,
    tail_frames,
):
    dp_count = lax.axis_size("dp")
    place = lax.axis_index("dp")
    core = lax.axis_index("fsdp") % 2
    rows, width = inputs.shape[2:]
    blocks = rows // BLOCK
    scale = 1.0 / math.sqrt(rows * lax.axis_size(("dp", "fsdp")))
    full_in = lax.all_gather(weight_in, "fsdp", axis=0, tiled=True)
    full_out = lax.all_gather(weight_out, "fsdp", axis=0, tiled=True)
    meta = scalars(pack_dest[0], utt_blocks[0], tail_frames[0], place, blocks)
    order = target_order(pack_dest[0], place, blocks)
    gain_in = norm_gain.reshape(1, width)
    gain_conv = conv_gain.reshape(1, width)

    quarters = spread(inputs.reshape(dp_count, rows // dp_count, width), "dp")
    arrived = spread(reorder(order, quarters), "dp")

    normed_in, inverse_in, gate, gate_slope, glu, low, high = project(
        meta, arrived, gain_in, full_in
    )
    glu_edges = halves_of_neighbours(low, high)
    held = conv_forward(True, meta, glu, kernel, gain_conv)
    normed, inverse, slope, swished = conv_forward(
        False, meta, glu, kernel, gain_conv, glu_edges, held
    )

    upstream = out_grad[0, 0]
    grad_s = lax.dot_general(
        upstream, full_out, (((1,), (1,)), ((), ())), preferred_element_type=F32
    )
    both = outer_of_chip(swished, upstream, core)
    both, grad_s = lax.optimization_barrier((both, grad_s))
    grad_conv, low, high = grad_conv_call(meta, normed, inverse, slope, grad_s)
    edges = halves_of_neighbours(low, high)
    both, grad_conv, edges = lax.optimization_barrier((both, grad_conv, edges))
    sent = send_over_dp(both)
    fsdp_count = lax.axis_size("fsdp")
    taps_rows = taps_gradient(meta, glu, grad_conv, glu_edges, fsdp_count, scale)
    taps_rows = sum_of_chip(taps_rows, core)
    taps_rows, grad_conv = lax.optimization_barrier((taps_rows, grad_conv))
    grad_proj = conv_backward(meta, grad_conv, kernel, gate, gate_slope, edges)
    taps_rows = sum_along_x(taps_rows)
    taps_rows, grad_proj, swished = lax.optimization_barrier((taps_rows, grad_proj, swished))
    module_out = multiply(swished, full_out)
    taps_rows, sent, module_out = lax.optimization_barrier((taps_rows, sent, module_out))
    pieces = summed_over_dp(sent, scale)
    taps_rows = sum_of_four(taps_rows, "dp", 1)
    taps_rows = sum_of_four(taps_rows, "dp", 4)
    taps_rows, pieces, grad_proj = lax.optimization_barrier((taps_rows, pieces, grad_proj))
    got = last_exchange(taps_rows, pieces)
    kernel_grad, weight_out_grad = after_exchange(got, TAPS // fsdp_count)
    input_grad = input_gradient(gain_in, grad_proj, full_in, normed_in, inverse_in)
    return (
        module_out.reshape(1, 1, rows, width),
        input_grad.reshape(1, 1, rows, width),
        weight_out_grad,
        kernel_grad,
    )


def solution(mesh):
    in_specs = (
        P("dp", "fsdp", None, None),
        P(),
        P("fsdp", None),
        P(),
        P(),
        P("fsdp", None),
        P("dp", "fsdp", None, None),
        P("fsdp", None),
        P("fsdp", None),
        P("fsdp", None),
    )
    out_specs = (
        P("dp", "fsdp", None, None),
        P("dp", "fsdp", None, None),
        P(("dp", "fsdp"), None),
        P(),
    )
    return jax.shard_map(local, mesh=mesh, in_specs=in_specs, out_specs=out_specs, check_vma=False)
```

```python
import functools
import math

import jax
import jax.numpy as jnp
from jax import lax
from jax.experimental import pallas as pl
from jax.experimental.pallas import tpu as pltpu
from jax.sharding import PartitionSpec as P

BLOCK = 128
LANES = 128
HALF = 16
TAPS = 32
EPS = 1e-05
VMEM = 28 * 2**20
F32 = jnp.float32
BF16 = jnp.bfloat16

LEFT, RIGHT, COUNT, SLOT = 0, 4, 8, 12


def row_mean(values):
    return jnp.mean(values, axis=-1, keepdims=True)


def normalise(values):
    centered = values - row_mean(values)
    inverse = lax.rsqrt(row_mean(centered * centered) + EPS)
    return centered * inverse, inverse


def below(count, rows, first=0):
    return lax.broadcasted_iota(jnp.int32, (rows, 1), 0) + first < count


def in_hbm(x):
    return pltpu.with_memory_space_constraint(x, pltpu.HBM)


def in_vmem(x):
    return pltpu.with_memory_space_constraint(x, pltpu.VMEM)


def params():
    return pltpu.CompilerParams(vmem_limit_bytes=VMEM)


def cost():
    return pl.CostEstimate(flops=1000, bytes_accessed=1000, transcendentals=0)


def whole(shape):
    return pl.BlockSpec(shape, lambda *_: (0,) * len(shape))


def reorder_kernel(order, x_ref, o_ref):
    for t in range(x_ref.shape[0]):
        o_ref[t] = x_ref[order[t]]


def reorder(order, x):
    return pl.pallas_call(
        reorder_kernel,
        out_shape=pltpu.HBM(x.shape, x.dtype),
        grid_spec=pltpu.PrefetchScalarGridSpec(
            num_scalar_prefetch=1,
            grid=(1,),
            in_specs=[whole(x.shape)],
            out_specs=whole(x.shape),
        ),
        compiler_params=params(),
        cost_estimate=cost(),
        name="reorder",
    )(order, in_vmem(x))


def tiles(width):
    return [slice(at, at + LANES) for at in range(0, width, LANES)]


def row_total(parts):
    return jnp.sum(functools.reduce(lambda a, b: a + b, parts), axis=1, keepdims=True)


def row_stats(load, width):
    mean = row_total(load(t) for t in tiles(width)) * (1.0 / width)

    def squared(t):
        centered = load(t) - mean
        return centered * centered

    var = row_total(squared(t) for t in tiles(width)) * (1.0 / width)
    return mean, lax.rsqrt(var + EPS)


def project_kernel(
    meta, x_ref, gain_ref, wl_ref, wg_ref,
    normed_ref, inverse_ref, gate_ref, slope_ref, glu_ref, low_ref, high_ref, hidden,
):
    count, quarter, width = x_ref.shape
    blocks = count * quarter // BLOCK
    quarters = count // blocks

    @pl.when(pl.program_id(0) == 0)
    def _():
        for j in range(blocks):
            rows = slice(j * BLOCK, (j + 1) * BLOCK)
            first = meta[SLOT + j] * quarters

            def load(t, first=first):
                return jnp.concatenate([x_ref[first + q, :, t] for q in range(quarters)]).astype(F32)

            mean, inverse = row_stats(load, width)
            inverse_ref[rows] = inverse
            for t in tiles(width):
                normed = (load(t) - mean) * inverse
                normed_ref[rows, t] = normed.astype(BF16)
                hidden[rows, t] = (normed * gain_ref[:, t]).astype(BF16)

    held = hidden[...]
    lin = jnp.dot(held, wl_ref[...], preferred_element_type=F32)
    gate = jax.nn.sigmoid(jnp.dot(held, wg_ref[...], preferred_element_type=F32))
    product = lin * gate
    gate_ref[...] = gate
    slope_ref[...] = product * (1.0 - gate)
    for j in range(blocks):
        rows = slice(j * BLOCK, (j + 1) * BLOCK)
        glu = jnp.where(below(meta[COUNT + j], BLOCK), product[rows], 0.0).astype(BF16)
        glu_ref[rows] = glu
        if j == 0:
            low_ref[...] = glu[:HALF]
        if j == blocks - 1:
            high_ref[...] = glu[BLOCK - HALF :]


def project(meta, x, gain, weight, tile=512):
    count, quarter, width = x.shape
    rows = count * quarter
    steps = width // tile
    column = pl.BlockSpec((rows, tile), lambda n, _: (0, n))
    edge = pl.BlockSpec((HALF, tile), lambda n, _: (0, n))
    return pl.pallas_call(
        project_kernel,
        out_shape=[
            pltpu.HBM((rows, width), BF16),
            pltpu.HBM((rows, 1), F32),
            pltpu.HBM((rows, width), F32),
            pltpu.HBM((rows, width), F32),
            jax.ShapeDtypeStruct((rows, width), BF16),
            pltpu.HBM((HALF, width), BF16),
            pltpu.HBM((HALF, width), BF16),
        ],
        grid_spec=pltpu.PrefetchScalarGridSpec(
            num_scalar_prefetch=1,
            grid=(steps,),
            in_specs=[
                whole(x.shape),
                whole((1, width)),
                pl.BlockSpec((width, tile), lambda n, _: (0, n)),
                pl.BlockSpec((width, tile), lambda n, _: (0, n + steps)),
            ],
            out_specs=[whole((rows, width)), whole((rows, 1)), column, column, column, edge, edge],
            scratch_shapes=[pltpu.VMEM((rows, width), BF16)],
        ),
        compiler_params=params(),
        cost_estimate=cost(),
        name="project",
    )(meta, in_hbm(x), gain, in_hbm(weight), in_hbm(weight))


def fill(pad, left, middle, right, left_ok, right_ok):
    pad[0:HALF] = jnp.where(left_ok > 0, left.astype(F32), 0.0)
    pad[HALF : HALF + BLOCK] = middle.astype(F32)
    pad[HALF + BLOCK :] = jnp.where(right_ok > 0, right.astype(F32), 0.0)


def fill_inner(pad, meta, b, src):
    at = pl.multiple_of(b * BLOCK, BLOCK)
    fill(
        pad,
        src[pl.ds(pl.multiple_of(at - HALF, HALF), HALF)],
        src[pl.ds(at, BLOCK)],
        src[pl.ds(pl.multiple_of(at + BLOCK, BLOCK), HALF)],
        meta[LEFT + b],
        meta[RIGHT + b],
    )


def fill_first(pad, meta, src, low):
    fill(pad, low[...], src[0:BLOCK], src[BLOCK : BLOCK + HALF], meta[LEFT], meta[RIGHT])


def fill_last(pad, meta, src, high):
    rows = src.shape[0]
    last = rows // BLOCK - 1
    fill(
        pad,
        src[rows - BLOCK - HALF : rows - BLOCK],
        src[rows - BLOCK :],
        high[...],
        meta[LEFT + last],
        meta[RIGHT + last],
    )


def slabs(pad, lanes, first):
    for p in range(8):
        offsets = [o for o in range(first, first + TAPS) if o % 8 == p]
        count = BLOCK + 8 * (offsets[-1] // 8)
        yield pad[pl.ds(p, count), lanes].reshape(count // 8, 8, LANES), offsets


def depthwise(pad, taps, lanes, first, tap_of):
    count = BLOCK // 8 + 1
    padded = pad[:, lanes].reshape(pad.shape[0] // 8, 8, LANES)
    total = None
    for p in range(8):
        offsets = [o for o in range(first, first + TAPS) if o % 8 == p]
        part = None
        for o in offsets:
            i = tap_of(o)
            rows = count if p else count - 1
            term = padded[o // 8 : o // 8 + rows] * taps[i : i + 1, lanes][None]
            part = term if part is None else part + term
        part = part.reshape(-1, LANES)
        if p:
            part = pltpu.roll(part, part.shape[0] - p, 0)[:BLOCK]
        total = part if total is None else total + part
    return total


def lane_tiles(width):
    return lambda body: pl.loop(0, width // LANES)(
        lambda c: body(pl.ds(pl.multiple_of(c * LANES, LANES), LANES))
    )


def pad_by_step(inner, meta, src, low, high, pad):
    step = pl.program_id(0)
    if inner:
        b = step + 1
        fill_inner(pad, meta, b, src)
        return b

    @pl.when(step == 0)
    def _():
        fill_first(pad, meta, src, low)

    @pl.when(step == 1)
    def _():
        fill_last(pad, meta, src, high)

    return step * (src.shape[0] // BLOCK - 1)


def conv_kernel(inner, meta, *refs):
    if inner:
        src, taps, gain, normed_ref, inverse_ref, slope_ref, swished_ref, pad, conv = refs
        low = high = None
    else:
        src, taps, gain, low, high, _, _, _, _, *refs = refs
        normed_ref, inverse_ref, slope_ref, swished_ref, pad, conv = refs
    width = src.shape[1]
    b = pad_by_step(inner, meta, src, low, high, pad)
    valid = below(meta[COUNT + b], BLOCK)

    @lane_tiles(width)
    def _(lanes):
        conv[:, lanes] = jnp.where(valid, depthwise(pad, taps, lanes, 0, lambda o: o), 0.0)

    mean, inverse = row_stats(lambda t: conv[:, t], width)
    inverse_ref[...] = inverse
    for t in tiles(width):
        normed = (conv[:, t] - mean) * inverse
        scaled = normed * gain[:, t]
        sig = jax.nn.sigmoid(scaled)
        swished = scaled * sig
        normed_ref[:, t] = normed.astype(BF16)
        swished_ref[:, t] = swished.astype(BF16)
        slope_ref[:, t] = (sig + swished * (1.0 - sig)) * gain[:, t]


def split_call(kernel, inner, meta, operands, edges, held, outs, width, flops):
    rows = operands[0].shape[0]
    last = rows // BLOCK - 1

    def place(n, _):
        return (n + 1 if inner else n * last, 0)

    in_specs = []
    for a in operands:
        if a.shape[0] == rows and a is not operands[0]:
            in_specs.append(pl.BlockSpec((BLOCK, a.shape[1]), place))
        else:
            in_specs.append(whole(a.shape))
    args = list(operands)
    aliases = {}
    if not inner:
        args += map(in_hbm, edges)
        in_specs += [whole(e.shape) for e in edges]
        for n, h in enumerate(held):
            aliases[1 + len(args)] = n
            args.append(h)
            in_specs.append(pl.BlockSpec(memory_space=pl.ANY))
    return pl.pallas_call(
        functools.partial(kernel, inner),
        out_shape=[jax.ShapeDtypeStruct(*o) for o in outs],
        grid_spec=pltpu.PrefetchScalarGridSpec(
            num_scalar_prefetch=1,
            grid=(2,),
            in_specs=in_specs,
            out_specs=[pl.BlockSpec((BLOCK, o[0][1]), place) for o in outs],
            scratch_shapes=[
                pltpu.VMEM((BLOCK + 2 * HALF, width), F32),
                pltpu.VMEM((BLOCK, width), F32),
            ],
        ),
        input_output_aliases=aliases,
        compiler_params=params(),
        cost_estimate=cost(),
        name=kernel.__name__ + ("_inner" if inner else "_edges"),
    )(meta, *args)


def conv_forward(inner, meta, glu, taps, gain, edges=(), held=()):
    rows, width = glu.shape
    return split_call(
        conv_kernel,
        inner,
        meta,
        (glu, taps, gain),
        edges,
        held,
        [((rows, width), BF16), ((rows, 1), F32), ((rows, width), F32), ((rows, width), BF16)],
        width,
        4 * 10**9,
    )


def multiply_kernel(x_ref, w_ref, out_ref):
    out_ref[...] = jnp.dot(x_ref[...], w_ref[...], preferred_element_type=F32).astype(BF16)


def multiply(x, weight, tile=512):
    rows, depth = x.shape
    width = weight.shape[1]
    return pl.pallas_call(
        multiply_kernel,
        out_shape=jax.ShapeDtypeStruct((rows, width), BF16),
        grid=(width // tile,),
        in_specs=[whole((rows, depth)), pl.BlockSpec((depth, tile), lambda n: (0, n))],
        out_specs=pl.BlockSpec((rows, tile), lambda n: (0, n)),
        compiler_params=params(),
        cost_estimate=cost(),
        name="multiply",
    )(x, in_hbm(weight))


def norm_back(load, normed_ref, inverse_ref, rows, width):
    normed = {t.start: normed_ref[rows, t].astype(F32) for t in tiles(width)}
    first = row_total(load(t) for t in tiles(width)) * (1.0 / width)
    second = row_total(load(t) * normed[t.start] for t in tiles(width)) * (1.0 / width)
    inverse = inverse_ref[rows]
    for t in tiles(width):
        yield t, (load(t) - first - normed[t.start] * second) * inverse


def grad_conv_kernel(
    meta, normed_ref, inverse_ref, slope_ref, grad_ref, out_ref, low_ref, high_ref
):
    b = pl.program_id(0)
    valid = below(meta[COUNT + b], BLOCK)
    for t, back in norm_back(
        lambda t: grad_ref[:, t] * slope_ref[:, t],
        normed_ref,
        inverse_ref,
        slice(None),
        normed_ref.shape[1],
    ):
        out_ref[:, t] = jnp.where(valid, back, 0.0).astype(BF16)

    @pl.when(b == 0)
    def _():
        low_ref[...] = out_ref[0:HALF]

    @pl.when(b == pl.num_programs(0) - 1)
    def _():
        high_ref[...] = out_ref[BLOCK - HALF :]


def grad_conv_call(meta, normed, inverse, slope, grad_s):
    rows, width = normed.shape
    block = pl.BlockSpec((BLOCK, width), lambda n, _: (n, 0))
    return pl.pallas_call(
        grad_conv_kernel,
        out_shape=[
            pltpu.HBM((rows, width), BF16),
            pltpu.HBM((HALF, width), BF16),
            pltpu.HBM((HALF, width), BF16),
        ],
        grid_spec=pltpu.PrefetchScalarGridSpec(
            num_scalar_prefetch=1,
            grid=(rows // BLOCK,),
            in_specs=[block, pl.BlockSpec((BLOCK, 1), lambda n, _: (n, 0)), block, block],
            out_specs=[block, whole((HALF, width)), whole((HALF, width))],
        ),
        compiler_params=params(),
        cost_estimate=cost(),
        name="grad_conv",
    )(meta, normed, inverse, slope, grad_s)


def pad_by_block(meta, src, low, high, pad):
    b = pl.program_id(0)
    last = pl.num_programs(0) - 1

    @pl.when(b == 0)
    def _():
        fill_first(pad, meta, src, low)

    @pl.when(b == last)
    def _():
        fill_last(pad, meta, src, high)

    @pl.when((b > 0) & (b < last))
    def _():
        fill_inner(pad, meta, b, src)


def taps_kernel(scale, meta, src, grad_ref, low, high, out_ref, pad, total):
    b = pl.program_id(0)
    last = pl.num_programs(0) - 1
    width = src.shape[1]
    pad_by_block(meta, src, low, high, pad)

    @pl.when(b == 0)
    def _():
        total[...] = jnp.zeros_like(total)

    @lane_tiles(width)
    def _(lanes):
        grad = grad_ref[:, lanes].astype(F32).reshape(BLOCK // 8, 8, LANES)
        for slab, offsets in slabs(pad, lanes, 0):
            for o in offsets:
                total[o, :, lanes] += jnp.sum(
                    slab[o // 8 : o // 8 + BLOCK // 8] * grad, axis=0
                )

    @pl.when(b == last)
    def _():
        groups, few = out_ref.shape[0], out_ref.shape[1] // 2
        half = width // 2
        for g in range(groups):
            own = jnp.sum(total[g * few : (g + 1) * few], axis=1) * scale
            out_ref[g, :few] = own[:, :half]
            out_ref[g, few:] = own[:, half:]


def taps_gradient(meta, glu, grad_conv, edges, groups, scale):
    rows, width = glu.shape
    return pl.pallas_call(
        functools.partial(taps_kernel, scale),
        out_shape=jax.ShapeDtypeStruct((groups, 2 * TAPS // groups, width // 2), F32),
        grid_spec=pltpu.PrefetchScalarGridSpec(
            num_scalar_prefetch=1,
            grid=(rows // BLOCK,),
            in_specs=[
                whole(glu.shape),
                pl.BlockSpec((BLOCK, width), lambda n, _: (n, 0)),
                whole((HALF, width)),
                whole((HALF, width)),
            ],
            out_specs=whole((groups, 2 * TAPS // groups, width // 2)),
            scratch_shapes=[
                pltpu.VMEM((BLOCK + 2 * HALF, width), F32),
                pltpu.VMEM((TAPS, 8, width), F32),
            ],
        ),
        compiler_params=params(),
        cost_estimate=cost(),
        name="taps_gradient",
    )(meta, glu, in_hbm(grad_conv), *map(in_hbm, edges))


def back_kernel(meta, src, taps, gate_ref, slope_ref, low, high, out_ref, pad):
    b = pl.program_id(0)
    width = src.shape[1]
    pad_by_block(meta, src, low, high, pad)
    valid = below(meta[COUNT + b], BLOCK)

    @pl.loop(0, width // LANES)
    def _(c):
        at = pl.multiple_of(c * LANES, LANES)
        lanes = pl.ds(at, LANES)
        grad = jnp.where(valid, depthwise(pad, taps, lanes, 1, lambda o: TAPS - o), 0.0)
        out_ref[:, lanes] = (grad * gate_ref[:, lanes]).astype(BF16)
        out_ref[:, pl.ds(pl.multiple_of(at + width, LANES), LANES)] = (
            grad * slope_ref[:, lanes]
        ).astype(BF16)


def conv_backward(meta, grad_conv, taps, gate, slope, edges):
    rows, width = grad_conv.shape
    block = pl.BlockSpec((BLOCK, width), lambda n, _: (n, 0))
    return pl.pallas_call(
        back_kernel,
        out_shape=pltpu.HBM((rows, 2 * width), BF16),
        grid_spec=pltpu.PrefetchScalarGridSpec(
            num_scalar_prefetch=1,
            grid=(rows // BLOCK,),
            in_specs=[
                whole(grad_conv.shape),
                whole(taps.shape),
                block,
                block,
                whole((HALF, width)),
                whole((HALF, width)),
            ],
            out_specs=pl.BlockSpec((BLOCK, 2 * width), lambda n, _: (n, 0)),
            scratch_shapes=[pltpu.VMEM((BLOCK + 2 * HALF, width), F32)],
        ),
        compiler_params=params(),
        cost_estimate=cost(),
        name="conv_backward",
    )(meta, in_hbm(grad_conv), taps, in_hbm(gate), in_hbm(slope), *map(in_hbm, edges))


def input_kernel(gain_ref, grad_ref, w_ref, normed_ref, inverse_ref, out_ref, hidden):
    n = pl.program_id(0)
    rows, width = hidden.shape
    tile = w_ref.shape[0]
    at = pl.ds(pl.multiple_of(n * tile, tile), tile)
    hidden[:, at] = gain_ref[:, at] * lax.dot_general(
        grad_ref[...], w_ref[...], (((1,), (1,)), ((), ())), preferred_element_type=F32
    )

    @pl.when(n == pl.num_programs(0) - 1)
    def _():
        for at in range(0, rows, BLOCK):
            part = slice(at, at + BLOCK)
            for t, back in norm_back(
                lambda t, part=part: hidden[part, t], normed_ref, inverse_ref, part, width
            ):
                out_ref[part, t] = back.astype(BF16)


def input_gradient(gain, grad_proj, weight, normed, inverse, tile=512):
    rows = grad_proj.shape[0]
    width = weight.shape[0]
    return pl.pallas_call(
        input_kernel,
        out_shape=jax.ShapeDtypeStruct((rows, width), BF16),
        grid=(width // tile,),
        in_specs=[
            whole((1, width)),
            whole(grad_proj.shape),
            pl.BlockSpec((tile, weight.shape[1]), lambda n: (n, 0)),
            whole(normed.shape),
            whole(inverse.shape),
        ],
        out_specs=whole((rows, width)),
        scratch_shapes=[pltpu.VMEM((rows, width), F32)],
        compiler_params=params(),
        cost_estimate=cost(),
        name="input_gradient",
    )(gain, in_hbm(grad_proj), in_hbm(weight), in_hbm(normed), in_hbm(inverse))


def halves_of_neighbours(low, high):
    count = lax.axis_size("dp")
    forward = [(i, i + 1) for i in range(count - 1)]
    backward = [(i + 1, i) for i in range(count - 1)]
    return lax.ppermute(high, "dp", forward), lax.ppermute(low, "dp", backward)


def swap(values, axis, bits):
    return lax.ppermute(values, axis, [(i, i ^ bits) for i in range(lax.axis_size(axis))])


def sum_of_four(values, axis, low_bit):
    one, two = low_bit, 2 * low_bit
    first, second, third = (swap(values, axis, b) for b in (one, two, one + two))
    return (values + first) + (second + third)


def sum_of_chip(groups, core):
    groups = groups.reshape((groups.shape[0] // 2, 2) + groups.shape[1:])
    other = lax.dynamic_index_in_dim(groups, 1 - core, axis=1, keepdims=False)
    own = lax.dynamic_index_in_dim(groups, core, axis=1, keepdims=False)
    return own + swap(other, "fsdp", 1)


def sum_along_x(groups):
    mine = lax.axis_index("fsdp") // 2
    total = lax.dynamic_index_in_dim(groups, mine, keepdims=False)
    for bits in range(1, groups.shape[0]):
        theirs = lax.dynamic_index_in_dim(groups, mine ^ bits, keepdims=False)
        total = total + swap(theirs, "fsdp", 2 * bits)
    return total


def spread(values, axis):
    return lax.all_to_all(values, axis, split_axis=0, concat_axis=0, tiled=True)


def outer(left, right):
    return lax.dot_general(left, right, (((0,), (0,)), ((), ())), preferred_element_type=F32)


def outer_of_chip(left, right, core):
    half = right.shape[1] // 2
    ours = lax.dynamic_slice_in_dim(right, core * half, half, axis=1)
    theirs = lax.dynamic_slice_in_dim(right, (1 - core) * half, half, axis=1)
    arrived = swap(outer(left, theirs).astype(BF16), "fsdp", 1)
    return (outer(left, ours) + arrived.astype(F32)).astype(BF16)


def send_over_dp(both):
    count = lax.axis_size("dp")
    return spread(both.reshape((count, both.shape[0] // count) + both.shape[1:]), "dp")


def summed_over_dp(sent, scale):
    total = jnp.sum(sent.astype(F32), axis=0) * scale
    count = lax.axis_size("fsdp")
    return total.reshape((count, total.shape[0] // count) + total.shape[1:])


def last_exchange(taps_rows, pieces):
    taps_rows = jnp.broadcast_to(taps_rows[None], pieces.shape[:1] + taps_rows.shape)
    return spread(jnp.concatenate([taps_rows, pieces], axis=1), "fsdp")


def after_exchange(got, few):
    count, _, half = got.shape
    left = got[:, :few].reshape(count * few, half)
    right = got[:, few : 2 * few].reshape(count * few, half)
    pieces = got[:, 2 * few :]
    pieces = jnp.sum(pieces.reshape((count // 2, 2) + pieces.shape[1:]), axis=0)
    return (
        jnp.concatenate([left, right], axis=1),
        jnp.concatenate([pieces[0], pieces[1]], axis=1),
    )


def scalars(packing, counts, tails, place, blocks):
    mine = place * blocks + jnp.arange(blocks, dtype=jnp.int32)
    number = jnp.arange(counts.shape[0], dtype=jnp.int32)
    ends = jnp.sum(jnp.where(number[:, None] <= number[None, :], counts[:, None], 0), axis=0)
    opens = (ends - counts)[None, :] == mine[:, None]
    closes = (ends - 1)[None, :] == mine[:, None]
    left = 1 - jnp.sum(opens.astype(jnp.int32), axis=1)
    right = 1 - jnp.sum(closes.astype(jnp.int32), axis=1)
    valid = BLOCK + jnp.sum(jnp.where(closes, tails[None, :] - BLOCK, 0), axis=1)
    number = jnp.arange(packing.shape[0], dtype=jnp.int32)
    slot = jnp.sum(
        jnp.where(packing[None, :] == mine[:, None], number[None, :] % blocks, 0), axis=1
    )
    return jnp.concatenate([left, right, valid, slot]).astype(jnp.int32)


def target_order(packing, place, blocks):
    count = packing.shape[0] // blocks
    color = place // blocks
    number = jnp.arange(packing.shape[0], dtype=jnp.int32)
    chosen = (number % blocks == color)[None, :]
    goes = (packing // blocks)[None, :] == jnp.arange(count, dtype=jnp.int32)[:, None]
    return jnp.sum(jnp.where(chosen & goes, (number // blocks)[None, :], 0), axis=1)


def local(
    inputs,
    norm_gain,
    weight_in,
    kernel,
    conv_gain,
    weight_out,
    out_grad,
    pack_dest,
    utt_blocks,
    tail_frames,
):
    dp_count = lax.axis_size("dp")
    place = lax.axis_index("dp")
    core = lax.axis_index("fsdp") % 2
    rows, width = inputs.shape[2:]
    blocks = rows // BLOCK
    scale = 1.0 / math.sqrt(rows * lax.axis_size(("dp", "fsdp")))
    full_in = lax.all_gather(weight_in, "fsdp", axis=0, tiled=True)
    full_out = lax.all_gather(weight_out, "fsdp", axis=0, tiled=True)
    meta = scalars(pack_dest[0], utt_blocks[0], tail_frames[0], place, blocks)
    order = target_order(pack_dest[0], place, blocks)
    gain_in = norm_gain.reshape(1, width)
    gain_conv = conv_gain.reshape(1, width)

    quarters = spread(inputs.reshape(dp_count, rows // dp_count, width), "dp")
    arrived = spread(reorder(order, quarters), "dp")

    normed_in, inverse_in, gate, gate_slope, glu, low, high = project(
        meta, arrived, gain_in, full_in
    )
    glu_edges = halves_of_neighbours(low, high)
    held = conv_forward(True, meta, glu, kernel, gain_conv)
    normed, inverse, slope, swished = conv_forward(
        False, meta, glu, kernel, gain_conv, glu_edges, held
    )

    upstream = out_grad[0, 0]
    grad_s = lax.dot_general(
        upstream, full_out, (((1,), (1,)), ((), ())), preferred_element_type=F32
    )
    both = outer_of_chip(swished, upstream, core)
    both, grad_s = lax.optimization_barrier((both, grad_s))
    grad_conv, low, high = grad_conv_call(meta, normed, inverse, slope, grad_s)
    edges = halves_of_neighbours(low, high)
    both, grad_conv, edges = lax.optimization_barrier((both, grad_conv, edges))
    sent = send_over_dp(both)
    fsdp_count = lax.axis_size("fsdp")
    taps_rows = taps_gradient(meta, glu, grad_conv, glu_edges, fsdp_count, scale)
    taps_rows = sum_of_chip(taps_rows, core)
    taps_rows, grad_conv = lax.optimization_barrier((taps_rows, grad_conv))
    grad_proj = conv_backward(meta, grad_conv, kernel, gate, gate_slope, edges)
    taps_rows = sum_along_x(taps_rows)
    taps_rows, grad_proj, swished = lax.optimization_barrier((taps_rows, grad_proj, swished))
    module_out = multiply(swished, full_out)
    taps_rows, sent, module_out = lax.optimization_barrier((taps_rows, sent, module_out))
    pieces = summed_over_dp(sent, scale)
    taps_rows = sum_of_four(taps_rows, "dp", 1)
    taps_rows = sum_of_four(taps_rows, "dp", 4)
    taps_rows, pieces, grad_proj = lax.optimization_barrier((taps_rows, pieces, grad_proj))
    got = last_exchange(taps_rows, pieces)
    kernel_grad, weight_out_grad = after_exchange(got, TAPS // fsdp_count)
    input_grad = input_gradient(gain_in, grad_proj, full_in, normed_in, inverse_in)
    return (
        module_out.reshape(1, 1, rows, width),
        input_grad.reshape(1, 1, rows, width),
        weight_out_grad,
        kernel_grad,
    )


def solution(mesh):
    in_specs = (
        P("dp", "fsdp", None, None),
        P(),
        P("fsdp", None),
        P(),
        P(),
        P("fsdp", None),
        P("dp", "fsdp", None, None),
        P("fsdp", None),
        P("fsdp", None),
        P("fsdp", None),
    )
    out_specs = (
        P("dp", "fsdp", None, None),
        P("dp", "fsdp", None, None),
        P(("dp", "fsdp"), None),
        P(),
    )
    return jax.shard_map(local, mesh=mesh, in_specs=in_specs, out_specs=out_specs, check_vma=False)
```

```python
import functools
import math

import jax
import jax.numpy as jnp
from jax import lax
from jax.experimental import pallas as pl
from jax.experimental.pallas import tpu as pltpu
from jax.sharding import PartitionSpec as P

BLOCK = 128
LANES = 128
HALF = 16
TAPS = 32
EPS = 1e-05
F32 = jnp.float32
BF16 = jnp.bfloat16

LEFT, RIGHT, COUNT, SLOT, NEXT = 0, 4, 8, 12, 16


def row_mean(values):
    return jnp.mean(values, axis=-1, keepdims=True)


def normalise(values):
    centered = values - row_mean(values)
    inverse = lax.rsqrt(row_mean(centered * centered) + EPS)
    return centered * inverse, inverse


def below(count, rows, first=0):
    return lax.broadcasted_iota(jnp.int32, (rows, 1), 0) + first < count


def in_hbm(x):
    return pltpu.with_memory_space_constraint(x, pltpu.HBM)


def in_vmem(x):
    return pltpu.with_memory_space_constraint(x, pltpu.VMEM)


def params(mib):
    return pltpu.CompilerParams(vmem_limit_bytes=mib * 2**20)


def cost():
    return pl.CostEstimate(flops=1000, bytes_accessed=1000, transcendentals=0)


def whole(shape):
    return pl.BlockSpec(shape, lambda *_: (0,) * len(shape))


def reorder_kernel(order, x_ref, o_ref):
    for t in range(x_ref.shape[0]):
        o_ref[t] = x_ref[order[t]]


def reorder(order, x):
    return pl.pallas_call(
        reorder_kernel,
        out_shape=pltpu.HBM(x.shape, x.dtype),
        grid_spec=pltpu.PrefetchScalarGridSpec(
            num_scalar_prefetch=1,
            grid=(1,),
            in_specs=[whole(x.shape)],
            out_specs=whole(x.shape),
        ),
        compiler_params=params(8),
        cost_estimate=cost(),
        name="reorder",
    )(order, in_vmem(x))


def tiles(width):
    return [slice(at, at + LANES) for at in range(0, width, LANES)]


def row_total(parts):
    return jnp.sum(functools.reduce(lambda a, b: a + b, parts), axis=1, keepdims=True)


def row_stats(load, width):
    mean = row_total(load(t) for t in tiles(width)) * (1.0 / width)

    def squared(t):
        centered = load(t) - mean
        return centered * centered

    var = row_total(squared(t) for t in tiles(width)) * (1.0 / width)
    return mean, lax.rsqrt(var + EPS)


def project_kernel(
    meta, x_ref, gain_ref, wl_ref, wg_ref,
    normed_ref, inverse_ref, gate_ref, slope_ref, glu_ref, low_ref, high_ref, hidden,
):
    count, quarter, width = x_ref.shape
    blocks = count * quarter // BLOCK
    quarters = count // blocks

    @pl.when(pl.program_id(0) == 0)
    def _():
        for j in range(blocks):
            rows = slice(j * BLOCK, (j + 1) * BLOCK)
            first = meta[SLOT + j] * quarters

            def load(t, first=first):
                return jnp.concatenate([x_ref[first + q, :, t] for q in range(quarters)]).astype(F32)

            mean, inverse = row_stats(load, width)
            inverse_ref[rows] = inverse
            for t in tiles(width):
                normed = (load(t) - mean) * inverse
                normed_ref[rows, t] = normed.astype(BF16)
                hidden[rows, t] = (normed * gain_ref[:, t]).astype(BF16)

    held = hidden[...]
    lin = jnp.dot(held, wl_ref[...], preferred_element_type=F32)
    gate = jax.nn.sigmoid(jnp.dot(held, wg_ref[...], preferred_element_type=F32))
    product = lin * gate
    gate_ref[...] = gate
    slope_ref[...] = product * (1.0 - gate)
    for j in range(blocks):
        rows = slice(j * BLOCK, (j + 1) * BLOCK)
        glu = jnp.where(below(meta[COUNT + j], BLOCK), product[rows], 0.0).astype(BF16)
        glu_ref[rows] = glu
        if j == 0:
            low_ref[...] = glu[: 2 * HALF]
        if j == blocks - 1:
            high_ref[...] = glu[BLOCK - 2 * HALF :]


def project(meta, x, gain, weight, tile=512):
    count, quarter, width = x.shape
    rows = count * quarter
    steps = width // tile
    column = pl.BlockSpec((rows, tile), lambda n, _: (0, n))
    edge = pl.BlockSpec((2 * HALF, tile), lambda n, _: (0, n))
    return pl.pallas_call(
        project_kernel,
        out_shape=[
            pltpu.HBM((rows, width), BF16),
            pltpu.HBM((rows, 1), F32),
            pltpu.HBM((rows, width), F32),
            pltpu.HBM((rows, width), F32),
            jax.ShapeDtypeStruct((rows, width), BF16),
            pltpu.HBM((2 * HALF, width), BF16),
            pltpu.HBM((2 * HALF, width), BF16),
        ],
        grid_spec=pltpu.PrefetchScalarGridSpec(
            num_scalar_prefetch=1,
            grid=(steps,),
            in_specs=[
                whole(x.shape),
                whole((1, width)),
                pl.BlockSpec((width, tile), lambda n, _: (0, n)),
                pl.BlockSpec((width, tile), lambda n, _: (0, n + steps)),
            ],
            out_specs=[whole((rows, width)), whole((rows, 1)), column, column, column, edge, edge],
            scratch_shapes=[pltpu.VMEM((rows, width), BF16)],
        ),
        compiler_params=params(28),
        cost_estimate=cost(),
        name="project",
    )(meta, in_hbm(x), gain, in_hbm(weight), in_hbm(weight))


def fill(pad, left, middle, right, left_ok, right_ok):
    pad[0:HALF] = jnp.where(left_ok > 0, left.astype(F32), 0.0)
    pad[HALF : HALF + BLOCK] = middle.astype(F32)
    pad[HALF + BLOCK :] = jnp.where(right_ok > 0, right.astype(F32), 0.0)


def fill_inner(pad, meta, b, src):
    at = pl.multiple_of(b * BLOCK, BLOCK)
    fill(
        pad,
        src[pl.ds(pl.multiple_of(at - HALF, HALF), HALF)],
        src[pl.ds(at, BLOCK)],
        src[pl.ds(pl.multiple_of(at + BLOCK, BLOCK), HALF)],
        meta[LEFT + b],
        meta[RIGHT + b],
    )


def fill_first(pad, meta, src, low):
    fill(pad, low, src[0:BLOCK], src[BLOCK : BLOCK + HALF], meta[LEFT], meta[RIGHT])


def fill_last(pad, meta, src, high):
    rows = src.shape[0]
    last = rows // BLOCK - 1
    fill(
        pad,
        src[rows - BLOCK - HALF : rows - BLOCK],
        src[rows - BLOCK :],
        high,
        meta[LEFT + last],
        meta[RIGHT + last],
    )


def slabs(pad, lanes, first):
    for p in range(8):
        offsets = [o for o in range(first, first + TAPS) if o % 8 == p]
        count = BLOCK + 8 * (offsets[-1] // 8)
        yield pad[pl.ds(p, count), lanes].reshape(count // 8, 8, LANES), offsets


def depthwise(pad, taps, lanes, first, tap_of, block=BLOCK):
    count = block // 8 + 1
    padded = pad[:, lanes].reshape(pad.shape[0] // 8, 8, LANES)
    total = None
    for p in range(8):
        offsets = [o for o in range(first, first + TAPS) if o % 8 == p]
        part = None
        for o in offsets:
            i = tap_of(o)
            rows = count if p else count - 1
            term = padded[o // 8 : o // 8 + rows] * taps[i : i + 1, lanes][None]
            part = term if part is None else part + term
        part = part.reshape(-1, LANES)
        if p:
            part = pltpu.roll(part, part.shape[0] - p, 0)[:block]
        total = part if total is None else total + part
    return total


def lane_tiles(width):
    return lambda body: pl.loop(0, width // LANES)(
        lambda c: body(pl.ds(pl.multiple_of(c * LANES, LANES), LANES))
    )


def pad_by_step(inner, meta, src, low, high, pad, beyond):
    step = pl.program_id(0)
    if inner:
        b = step + 1
        fill_inner(pad, meta, b, src)
        return b
    rows = src.shape[0]

    @pl.when(step == 0)
    def _():
        fill_first(pad, meta, src, low[HALF:])
        beyond[: 2 * HALF] = low[...].astype(F32)
        beyond[2 * HALF :] = src[:HALF].astype(F32)

    @pl.when(step == 1)
    def _():
        fill_last(pad, meta, src, high[:HALF])
        beyond[:HALF] = src[rows - HALF :].astype(F32)
        beyond[HALF:] = high[...].astype(F32)

    return step * (rows // BLOCK - 1)


def activate(conv, gain, normed_ref, inverse_ref, slope_ref, swished_ref=None):
    width = conv.shape[1]
    mean, inverse = row_stats(lambda t: conv[:, t], width)
    inverse_ref[...] = inverse
    for t in tiles(width):
        normed = (conv[:, t] - mean) * inverse
        scaled = normed * gain[:, t]
        sig = jax.nn.sigmoid(scaled)
        swished = scaled * sig
        normed_ref[:, t] = normed.astype(BF16)
        slope_ref[:, t] = (sig + swished * (1.0 - sig)) * gain[:, t]
        if swished_ref is not None:
            swished_ref[:, t] = swished.astype(BF16)


def conv_kernel(inner, meta, *refs):
    if inner:
        src, taps, gain, *outs, pad, conv, beyond, far = refs
        low = high = None
    else:
        src, taps, gain, low, high, _, _, _, _, *outs, pad, conv, beyond, far = refs
    width = src.shape[1]
    b = pad_by_step(inner, meta, src, low, high, pad, beyond)
    valid = below(meta[COUNT + b], BLOCK)
    far_valid = below(jnp.where(pl.program_id(0) == 0, HALF, meta[NEXT]), HALF)

    @lane_tiles(width)
    def _(lanes):
        conv[:, lanes] = jnp.where(valid, depthwise(pad, taps, lanes, 0, lambda o: o), 0.0)
        if not inner:
            found = depthwise(beyond, taps, lanes, 0, lambda o: o, HALF)
            far[:, lanes] = jnp.where(far_valid, found, 0.0)

    activate(conv, gain, *outs[:4])
    if not inner:
        activate(far, gain, *outs[4:])


def split_call(kernel, inner, meta, operands, edges, held, outs, width, flops):
    rows = operands[0].shape[0]
    last = rows // BLOCK - 1

    def place(n, _):
        return (n + 1 if inner else n * last, 0)

    in_specs = []
    for a in operands:
        if a.shape[0] == rows and a is not operands[0]:
            in_specs.append(pl.BlockSpec((BLOCK, a.shape[1]), place))
        else:
            in_specs.append(whole(a.shape))
    args = list(operands)
    aliases = {}
    if not inner:
        args += map(in_hbm, edges)
        in_specs += [whole(e.shape) for e in edges]
        for n, h in enumerate(held):
            aliases[1 + len(args)] = n
            args.append(in_hbm(h) if outs[n][2] is pltpu.HBM else h)
            in_specs.append(pl.BlockSpec(memory_space=pl.ANY))
    return pl.pallas_call(
        functools.partial(kernel, inner),
        out_shape=[o[2](*o[:2]) for o in outs],
        grid_spec=pltpu.PrefetchScalarGridSpec(
            num_scalar_prefetch=1,
            grid=(2,),
            in_specs=in_specs,
            out_specs=[
                pl.BlockSpec((BLOCK, o[0][1]), place)
                if o[0][0] == rows
                else pl.BlockSpec((HALF, o[0][1]), lambda n, _: (n, 0))
                for o in outs
            ],
            scratch_shapes=[
                pltpu.VMEM((BLOCK + 2 * HALF, width), F32),
                pltpu.VMEM((BLOCK, width), F32),
                pltpu.VMEM((3 * HALF, width), F32),
                pltpu.VMEM((HALF, width), F32),
            ],
        ),
        input_output_aliases=aliases,
        compiler_params=params(16),
        cost_estimate=cost(),
        name=kernel.__name__ + ("_inner" if inner else "_edges"),
    )(meta, *args)


def conv_forward(inner, meta, glu, taps, gain, edges=(), held=()):
    rows, width = glu.shape
    outs = [
        ((rows, width), BF16, pltpu.HBM),
        ((rows, 1), F32, pltpu.HBM),
        ((rows, width), F32, pltpu.HBM),
        ((rows, width), BF16, jax.ShapeDtypeStruct),
    ]
    if not inner:
        outs += [((2 * HALF, o[0][1]), *o[1:]) for o in outs[:3]]
    return split_call(
        conv_kernel,
        inner,
        meta,
        (glu, taps, gain),
        edges,
        held,
        outs,
        width,
        4 * 10**9,
    )


def multiply_kernel(x_ref, w_ref, out_ref):
    out_ref[...] = jnp.dot(x_ref[...], w_ref[...], preferred_element_type=F32).astype(BF16)


def multiply(x, weight, tile=512):
    rows, depth = x.shape
    width = weight.shape[1]
    return pl.pallas_call(
        multiply_kernel,
        out_shape=jax.ShapeDtypeStruct((rows, width), BF16),
        grid=(width // tile,),
        in_specs=[whole((rows, depth)), pl.BlockSpec((depth, tile), lambda n: (0, n))],
        out_specs=pl.BlockSpec((rows, tile), lambda n: (0, n)),
        compiler_params=params(12),
        cost_estimate=cost(),
        name="multiply",
    )(x, in_hbm(weight))


def norm_back(load, normed_ref, inverse_ref, rows, width, first=None):
    normed = {t.start: normed_ref[rows, t].astype(F32) for t in tiles(width)}
    mean = row_total(load(t) for t in tiles(width)) * (1.0 / width)
    second = row_total(load(t) * normed[t.start] for t in tiles(width)) * (1.0 / width)
    if first is not None:
        rows = slice(first, first + rows.stop - rows.start)
    inverse = inverse_ref[rows]
    for t in tiles(width):
        yield t, (load(t) - mean - normed[t.start] * second) * inverse


def grad_conv_kernel(
    meta, grad_ref, w_ref, normed_ref, slope_ref, far_normed, far_slope, inverse_ref, far_inverse,
    out_ref, far_ref, incoming, normed,
):
    n = pl.program_id(0)
    rows, width = out_ref.shape
    tile = w_ref.shape[0]
    at = pl.ds(pl.multiple_of(n * tile, tile), tile)
    grad_s = lax.dot_general(
        grad_ref[...], w_ref[...], (((1,), (1,)), ((), ())), preferred_element_type=F32
    )
    incoming[:rows, at] = grad_s[:rows] * slope_ref[...]
    incoming[rows:, at] = grad_s[rows:] * far_slope[...]
    normed[:rows, at] = normed_ref[...]
    normed[rows:, at] = far_normed[...]

    def finish(ref, part, first, inverse, valid):
        count = part.stop - part.start
        for t, back in norm_back(
            lambda t: incoming[part, t], normed, inverse, part, width, first
        ):
            ref[first : first + count, t] = jnp.where(valid, back, 0.0).astype(BF16)

    @pl.when(n == pl.num_programs(0) - 1)
    def _():
        for b in range(rows // BLOCK):
            part = slice(b * BLOCK, (b + 1) * BLOCK)
            finish(out_ref, part, b * BLOCK, inverse_ref, below(meta[COUNT + b], BLOCK))
        part = slice(rows, rows + 2 * HALF)
        finish(far_ref, part, 0, far_inverse, below(HALF + meta[NEXT], 2 * HALF))


def grad_conv_call(meta, around, weight, normed, inverse, slope, far, tile=512):
    rows, width = normed.shape
    far_normed, far_inverse, far_slope = far
    column = pl.BlockSpec((rows, tile), lambda n, _: (0, n))
    beyond = pl.BlockSpec((2 * HALF, tile), lambda n, _: (0, n))
    return pl.pallas_call(
        grad_conv_kernel,
        out_shape=[pltpu.HBM((rows, width), BF16), pltpu.HBM((2 * HALF, width), BF16)],
        grid_spec=pltpu.PrefetchScalarGridSpec(
            num_scalar_prefetch=1,
            grid=(width // tile,),
            in_specs=[
                whole(around.shape),
                pl.BlockSpec((tile, width), lambda n, _: (n, 0)),
                column,
                column,
                beyond,
                beyond,
                whole(inverse.shape),
                whole(far_inverse.shape),
            ],
            out_specs=[whole((rows, width)), whole((2 * HALF, width))],
            scratch_shapes=[
                pltpu.VMEM((rows + 2 * HALF, width), F32),
                pltpu.VMEM((rows + 2 * HALF, width), BF16),
            ],
        ),
        compiler_params=params(28),
        cost_estimate=cost(),
        name="grad_conv",
    )(
        meta,
        around,
        in_hbm(weight),
        *map(in_hbm, (normed, slope, far_normed, far_slope, inverse, far_inverse)),
    )


def pad_by_block(meta, src, low, high, pad):
    b = pl.program_id(0)
    last = pl.num_programs(0) - 1

    @pl.when(b == 0)
    def _():
        fill_first(pad, meta, src, low())

    @pl.when(b == last)
    def _():
        fill_last(pad, meta, src, high())

    @pl.when((b > 0) & (b < last))
    def _():
        fill_inner(pad, meta, b, src)


def taps_kernel(scale, meta, src, grad_ref, low, high, out_ref, pad, total):
    b = pl.program_id(0)
    last = pl.num_programs(0) - 1
    width = src.shape[1]
    pad_by_block(meta, src, lambda: low[HALF:], lambda: high[:HALF], pad)

    @pl.when(b == 0)
    def _():
        total[...] = jnp.zeros_like(total)

    @lane_tiles(width)
    def _(lanes):
        grad = grad_ref[:, lanes].astype(F32).reshape(BLOCK // 8, 8, LANES)
        for slab, offsets in slabs(pad, lanes, 0):
            for o in offsets:
                total[o, :, lanes] += jnp.sum(
                    slab[o // 8 : o // 8 + BLOCK // 8] * grad, axis=0
                )

    @pl.when(b == last)
    def _():
        groups, few = out_ref.shape[0], out_ref.shape[1] // 2
        half = width // 2
        for g in range(groups):
            own = jnp.sum(total[g * few : (g + 1) * few], axis=1) * scale
            out_ref[g, :few] = own[:, :half]
            out_ref[g, few:] = own[:, half:]


def taps_gradient(meta, glu, grad_conv, edges, groups, scale):
    rows, width = glu.shape
    return pl.pallas_call(
        functools.partial(taps_kernel, scale),
        out_shape=jax.ShapeDtypeStruct((groups, 2 * TAPS // groups, width // 2), F32),
        grid_spec=pltpu.PrefetchScalarGridSpec(
            num_scalar_prefetch=1,
            grid=(rows // BLOCK,),
            in_specs=[
                whole(glu.shape),
                pl.BlockSpec((BLOCK, width), lambda n, _: (n, 0)),
                whole((2 * HALF, width)),
                whole((2 * HALF, width)),
            ],
            out_specs=whole((groups, 2 * TAPS // groups, width // 2)),
            scratch_shapes=[
                pltpu.VMEM((BLOCK + 2 * HALF, width), F32),
                pltpu.VMEM((TAPS, 8, width), F32),
            ],
        ),
        compiler_params=params(16),
        cost_estimate=cost(),
        name="taps_gradient",
    )(meta, glu, in_hbm(grad_conv), *map(in_hbm, edges))


def back_kernel(meta, src, taps, gate_ref, slope_ref, far, out_ref, pad):
    b = pl.program_id(0)
    width = src.shape[1]
    pad_by_block(meta, src, lambda: far[:HALF], lambda: far[HALF:], pad)
    valid = below(meta[COUNT + b], BLOCK)

    @pl.loop(0, width // LANES)
    def _(c):
        at = pl.multiple_of(c * LANES, LANES)
        lanes = pl.ds(at, LANES)
        grad = jnp.where(valid, depthwise(pad, taps, lanes, 1, lambda o: TAPS - o), 0.0)
        out_ref[:, lanes] = (grad * gate_ref[:, lanes]).astype(BF16)
        out_ref[:, pl.ds(pl.multiple_of(at + width, LANES), LANES)] = (
            grad * slope_ref[:, lanes]
        ).astype(BF16)


def conv_backward(meta, grad_conv, far, taps, gate, slope):
    rows, width = grad_conv.shape
    block = pl.BlockSpec((BLOCK, width), lambda n, _: (n, 0))
    return pl.pallas_call(
        back_kernel,
        out_shape=pltpu.HBM((rows, 2 * width), BF16),
        grid_spec=pltpu.PrefetchScalarGridSpec(
            num_scalar_prefetch=1,
            grid=(rows // BLOCK,),
            in_specs=[
                whole(grad_conv.shape),
                whole(taps.shape),
                block,
                block,
                whole(far.shape),
            ],
            out_specs=pl.BlockSpec((BLOCK, 2 * width), lambda n, _: (n, 0)),
            scratch_shapes=[pltpu.VMEM((BLOCK + 2 * HALF, width), F32)],
        ),
        compiler_params=params(16),
        cost_estimate=cost(),
        name="conv_backward",
    )(meta, in_hbm(grad_conv), taps, in_hbm(gate), in_hbm(slope), in_hbm(far))


def input_kernel(gain_ref, grad_ref, w_ref, normed_ref, inverse_ref, out_ref, hidden):
    n = pl.program_id(0)
    rows, width = hidden.shape
    tile = w_ref.shape[0]
    at = pl.ds(pl.multiple_of(n * tile, tile), tile)
    hidden[:, at] = gain_ref[:, at] * lax.dot_general(
        grad_ref[...], w_ref[...], (((1,), (1,)), ((), ())), preferred_element_type=F32
    )

    @pl.when(n == pl.num_programs(0) - 1)
    def _():
        for at in range(0, rows, BLOCK):
            part = slice(at, at + BLOCK)
            for t, back in norm_back(
                lambda t, part=part: hidden[part, t], normed_ref, inverse_ref, part, width
            ):
                out_ref[part, t] = back.astype(BF16)


def input_gradient(gain, grad_proj, weight, normed, inverse, tile=512):
    rows = grad_proj.shape[0]
    width = weight.shape[0]
    return pl.pallas_call(
        input_kernel,
        out_shape=jax.ShapeDtypeStruct((rows, width), BF16),
        grid=(width // tile,),
        in_specs=[
            whole((1, width)),
            whole(grad_proj.shape),
            pl.BlockSpec((tile, weight.shape[1]), lambda n: (n, 0)),
            whole(normed.shape),
            whole(inverse.shape),
        ],
        out_specs=whole((rows, width)),
        scratch_shapes=[pltpu.VMEM((rows, width), F32)],
        compiler_params=params(28),
        cost_estimate=cost(),
        name="input_gradient",
    )(gain, in_hbm(grad_proj), in_hbm(weight), in_hbm(normed), in_hbm(inverse))


def halves_of_neighbours(low, high):
    count = lax.axis_size("dp")
    forward = [(i, i + 1) for i in range(count - 1)]
    backward = [(i + 1, i) for i in range(count - 1)]
    return lax.ppermute(high, "dp", forward), lax.ppermute(low, "dp", backward)


def swap(values, axis, bits):
    return lax.ppermute(values, axis, [(i, i ^ bits) for i in range(lax.axis_size(axis))])


def sum_of_four(values, axis, low_bit):
    one, two = low_bit, 2 * low_bit
    first, second, third = (swap(values, axis, b) for b in (one, two, one + two))
    return (values + first) + (second + third)


def sum_of_chip(groups, core):
    groups = groups.reshape((groups.shape[0] // 2, 2) + groups.shape[1:])
    other = lax.dynamic_index_in_dim(groups, 1 - core, axis=1, keepdims=False)
    own = lax.dynamic_index_in_dim(groups, core, axis=1, keepdims=False)
    return own + swap(other, "fsdp", 1)


def sum_along_x(groups):
    mine = lax.axis_index("fsdp") // 2
    total = lax.dynamic_index_in_dim(groups, mine, keepdims=False)
    for bits in range(1, groups.shape[0]):
        theirs = lax.dynamic_index_in_dim(groups, mine ^ bits, keepdims=False)
        total = total + swap(theirs, "fsdp", 2 * bits)
    return total


def spread(values, axis):
    return lax.all_to_all(values, axis, split_axis=0, concat_axis=0, tiled=True)


def outer(left, right):
    return lax.dot_general(left, right, (((0,), (0,)), ((), ())), preferred_element_type=F32)


def half_of(values, which):
    half = values.shape[1] // 2
    return lax.dynamic_slice_in_dim(values, which * half, half, axis=1)


def half_for_other(left, right, core):
    return swap(outer(left, half_of(right, 1 - core)).astype(BF16), "fsdp", 1)


def with_own_half(left, right, core, arrived):
    return (outer(left, half_of(right, core)) + arrived.astype(F32)).astype(BF16)


def send_over_dp(both):
    count = lax.axis_size("dp")
    return spread(both.reshape((count, both.shape[0] // count) + both.shape[1:]), "dp")


def summed_over_dp(sent, scale):
    total = jnp.sum(sent.astype(F32), axis=0) * scale
    count = lax.axis_size("fsdp")
    return total.reshape((count, total.shape[0] // count) + total.shape[1:])


def last_exchange(taps_rows, pieces):
    taps_rows = jnp.broadcast_to(taps_rows[None], pieces.shape[:1] + taps_rows.shape)
    return spread(jnp.concatenate([taps_rows, pieces], axis=1), "fsdp")


def after_exchange(got, few):
    count, _, half = got.shape
    left = got[:, :few].reshape(count * few, half)
    right = got[:, few : 2 * few].reshape(count * few, half)
    pieces = got[:, 2 * few :]
    pieces = jnp.sum(pieces.reshape((count // 2, 2) + pieces.shape[1:]), axis=0)
    return (
        jnp.concatenate([left, right], axis=1),
        jnp.concatenate([pieces[0], pieces[1]], axis=1),
    )


def scalars(packing, counts, tails, place, blocks):
    mine = place * blocks + jnp.arange(blocks, dtype=jnp.int32)
    number = jnp.arange(counts.shape[0], dtype=jnp.int32)
    ends = jnp.sum(jnp.where(number[:, None] <= number[None, :], counts[:, None], 0), axis=0)
    opens = (ends - counts)[None, :] == mine[:, None]
    closes = (ends - 1)[None, :] == mine[:, None]
    left = 1 - jnp.sum(opens.astype(jnp.int32), axis=1)
    right = 1 - jnp.sum(closes.astype(jnp.int32), axis=1)
    valid = BLOCK + jnp.sum(jnp.where(closes, tails[None, :] - BLOCK, 0), axis=1)
    number = jnp.arange(packing.shape[0], dtype=jnp.int32)
    slot = jnp.sum(
        jnp.where(packing[None, :] == mine[:, None], number[None, :] % blocks, 0), axis=1
    )
    closes = ends - 1 == (place + 1) * blocks
    after = BLOCK + jnp.sum(jnp.where(closes, tails - BLOCK, 0), keepdims=True)
    return jnp.concatenate([left, right, valid, slot, after]).astype(jnp.int32)


def target_order(packing, place, blocks):
    count = packing.shape[0] // blocks
    color = place // blocks
    number = jnp.arange(packing.shape[0], dtype=jnp.int32)
    chosen = (number % blocks == color)[None, :]
    goes = (packing // blocks)[None, :] == jnp.arange(count, dtype=jnp.int32)[:, None]
    return jnp.sum(jnp.where(chosen & goes, (number // blocks)[None, :], 0), axis=1)


def local(
    inputs,
    norm_gain,
    weight_in,
    kernel,
    conv_gain,
    weight_out,
    out_grad,
    pack_dest,
    utt_blocks,
    tail_frames,
):
    dp_count = lax.axis_size("dp")
    place = lax.axis_index("dp")
    core = lax.axis_index("fsdp") % 2
    rows, width = inputs.shape[2:]
    blocks = rows // BLOCK
    scale = 1.0 / math.sqrt(rows * lax.axis_size(("dp", "fsdp")))
    full_in = lax.all_gather(weight_in, "fsdp", axis=0, tiled=True)
    full_out = lax.all_gather(weight_out, "fsdp", axis=0, tiled=True)
    meta = scalars(pack_dest[0], utt_blocks[0], tail_frames[0], place, blocks)
    order = target_order(pack_dest[0], place, blocks)
    gain_in = norm_gain.reshape(1, width)
    gain_conv = conv_gain.reshape(1, width)

    quarters = spread(inputs.reshape(dp_count, rows // dp_count, width), "dp")
    upstream = out_grad[0, 0]
    beyond = halves_of_neighbours(upstream[:HALF], upstream[rows - HALF :])
    order, beyond = lax.optimization_barrier((order, beyond))
    around = jnp.concatenate([upstream, *beyond])
    arrived = spread(reorder(order, quarters), "dp")

    normed_in, inverse_in, gate, gate_slope, glu, low, high = project(
        meta, arrived, gain_in, full_in
    )
    glu_edges = halves_of_neighbours(low, high)
    held = conv_forward(True, meta, glu, kernel, gain_conv)
    normed, inverse, slope, swished, *far = conv_forward(
        False, meta, glu, kernel, gain_conv, glu_edges, held
    )

    arrived = half_for_other(swished, upstream, core)
    grad_conv, far = grad_conv_call(meta, around, full_out, normed, inverse, slope, far)
    arrived, grad_conv = lax.optimization_barrier((arrived, grad_conv))
    both = with_own_half(swished, upstream, core, arrived)
    sent = send_over_dp(both)
    fsdp_count = lax.axis_size("fsdp")
    taps_rows = taps_gradient(meta, glu, grad_conv, glu_edges, fsdp_count, scale)
    taps_rows = sum_of_chip(taps_rows, core)
    taps_rows, grad_conv = lax.optimization_barrier((taps_rows, grad_conv))
    grad_proj = conv_backward(meta, grad_conv, far, kernel, gate, gate_slope)
    taps_rows = sum_along_x(taps_rows)
    taps_rows, grad_proj, swished = lax.optimization_barrier((taps_rows, grad_proj, swished))
    module_out = multiply(swished, full_out)
    taps_rows, sent, module_out = lax.optimization_barrier((taps_rows, sent, module_out))
    pieces = summed_over_dp(sent, scale)
    taps_rows = sum_of_four(taps_rows, "dp", 1)
    taps_rows = sum_of_four(taps_rows, "dp", 4)
    taps_rows, pieces, grad_proj = lax.optimization_barrier((taps_rows, pieces, grad_proj))
    got = last_exchange(taps_rows, pieces)
    kernel_grad, weight_out_grad = after_exchange(got, TAPS // fsdp_count)
    input_grad = input_gradient(gain_in, grad_proj, full_in, normed_in, inverse_in)
    return (
        module_out.reshape(1, 1, rows, width),
        input_grad.reshape(1, 1, rows, width),
        weight_out_grad,
        kernel_grad,
    )


def solution(mesh):
    in_specs = (
        P("dp", "fsdp", None, None),
        P(),
        P("fsdp", None),
        P(),
        P(),
        P("fsdp", None),
        P("dp", "fsdp", None, None),
        P("fsdp", None),
        P("fsdp", None),
        P("fsdp", None),
    )
    out_specs = (
        P("dp", "fsdp", None, None),
        P("dp", "fsdp", None, None),
        P(("dp", "fsdp"), None),
        P(),
    )
    return jax.shard_map(local, mesh=mesh, in_specs=in_specs, out_specs=out_specs, check_vma=False)
```

```python
import functools
import math

import jax
import jax.numpy as jnp
from jax import lax
from jax.experimental import pallas as pl
from jax.experimental.pallas import tpu as pltpu
from jax.sharding import PartitionSpec as P

BLOCK = 128
LANES = 128
HALF = 16
TAPS = 32
EPS = 1e-05
F32 = jnp.float32
BF16 = jnp.bfloat16

LEFT, RIGHT, COUNT, SLOT, NEXT = 0, 4, 8, 12, 16


def row_mean(values):
    return jnp.mean(values, axis=-1, keepdims=True)


def normalise(values):
    centered = values - row_mean(values)
    inverse = lax.rsqrt(row_mean(centered * centered) + EPS)
    return centered * inverse, inverse


def below(count, rows, first=0):
    return lax.broadcasted_iota(jnp.int32, (rows, 1), 0) + first < count


def in_hbm(x):
    return pltpu.with_memory_space_constraint(x, pltpu.HBM)


def in_vmem(x):
    return pltpu.with_memory_space_constraint(x, pltpu.VMEM)


def params(mib):
    return pltpu.CompilerParams(vmem_limit_bytes=mib * 2**20)


def cost():
    return pl.CostEstimate(flops=1000, bytes_accessed=1000, transcendentals=0)


def whole(shape):
    return pl.BlockSpec(shape, lambda *_: (0,) * len(shape))


def reorder_kernel(order, x_ref, o_ref):
    for t in range(x_ref.shape[0]):
        o_ref[t] = x_ref[order[t]]


def reorder(order, x):
    return pl.pallas_call(
        reorder_kernel,
        out_shape=pltpu.HBM(x.shape, x.dtype),
        grid_spec=pltpu.PrefetchScalarGridSpec(
            num_scalar_prefetch=1,
            grid=(1,),
            in_specs=[whole(x.shape)],
            out_specs=whole(x.shape),
        ),
        compiler_params=params(8),
        cost_estimate=cost(),
        name="reorder",
    )(order, in_vmem(x))


def tiles(width):
    return [slice(at, at + LANES) for at in range(0, width, LANES)]


def row_total(parts):
    return jnp.sum(functools.reduce(lambda a, b: a + b, parts), axis=1, keepdims=True)


def row_stats(load, width):
    mean = row_total(load(t) for t in tiles(width)) * (1.0 / width)

    def squared(t):
        centered = load(t) - mean
        return centered * centered

    var = row_total(squared(t) for t in tiles(width)) * (1.0 / width)
    return mean, lax.rsqrt(var + EPS)


def project_kernel(
    meta, x_ref, gain_ref, wl_ref, wg_ref,
    normed_ref, inverse_ref, gate_ref, slope_ref, glu_ref, low_ref, high_ref, hidden,
):
    count, quarter, width = x_ref.shape
    blocks = count * quarter // BLOCK
    quarters = count // blocks

    @pl.when(pl.program_id(0) == 0)
    def _():
        for j in range(blocks):
            rows = slice(j * BLOCK, (j + 1) * BLOCK)
            first = meta[SLOT + j] * quarters

            def load(t, first=first):
                return jnp.concatenate([x_ref[first + q, :, t] for q in range(quarters)]).astype(F32)

            mean, inverse = row_stats(load, width)
            inverse_ref[rows] = inverse
            for t in tiles(width):
                normed = (load(t) - mean) * inverse
                normed_ref[rows, t] = normed.astype(BF16)
                hidden[rows, t] = (normed * gain_ref[:, t]).astype(BF16)

    held = hidden[...]
    lin = jnp.dot(held, wl_ref[...], preferred_element_type=F32)
    gate = jax.nn.sigmoid(jnp.dot(held, wg_ref[...], preferred_element_type=F32))
    product = lin * gate
    gate_ref[...] = gate
    slope_ref[...] = product * (1.0 - gate)
    for j in range(blocks):
        rows = slice(j * BLOCK, (j + 1) * BLOCK)
        glu = jnp.where(below(meta[COUNT + j], BLOCK), product[rows], 0.0).astype(BF16)
        glu_ref[rows] = glu
        if j == 0:
            low_ref[...] = glu[: 2 * HALF]
        if j == blocks - 1:
            high_ref[...] = glu[BLOCK - 2 * HALF :]


def project(meta, x, gain, weight, tile=512):
    count, quarter, width = x.shape
    rows = count * quarter
    steps = width // tile
    column = pl.BlockSpec((rows, tile), lambda n, _: (0, n))
    edge = pl.BlockSpec((2 * HALF, tile), lambda n, _: (0, n))
    return pl.pallas_call(
        project_kernel,
        out_shape=[
            pltpu.HBM((rows, width), BF16),
            pltpu.HBM((rows, 1), F32),
            pltpu.HBM((rows, width), F32),
            pltpu.HBM((rows, width), F32),
            jax.ShapeDtypeStruct((rows, width), BF16),
            pltpu.HBM((2 * HALF, width), BF16),
            pltpu.HBM((2 * HALF, width), BF16),
        ],
        grid_spec=pltpu.PrefetchScalarGridSpec(
            num_scalar_prefetch=1,
            grid=(steps,),
            in_specs=[
                whole(x.shape),
                whole((1, width)),
                pl.BlockSpec((width, tile), lambda n, _: (0, n)),
                pl.BlockSpec((width, tile), lambda n, _: (0, n + steps)),
            ],
            out_specs=[whole((rows, width)), whole((rows, 1)), column, column, column, edge, edge],
            scratch_shapes=[pltpu.VMEM((rows, width), BF16)],
        ),
        compiler_params=params(28),
        cost_estimate=cost(),
        name="project",
    )(meta, in_hbm(x), gain, in_hbm(weight), in_hbm(weight))


def fill(pad, left, middle, right, left_ok, right_ok):
    pad[0:HALF] = jnp.where(left_ok > 0, left.astype(F32), 0.0)
    pad[HALF : HALF + BLOCK] = middle.astype(F32)
    pad[HALF + BLOCK :] = jnp.where(right_ok > 0, right.astype(F32), 0.0)


def fill_inner(pad, meta, b, src):
    at = pl.multiple_of(b * BLOCK, BLOCK)
    fill(
        pad,
        src[pl.ds(pl.multiple_of(at - HALF, HALF), HALF)],
        src[pl.ds(at, BLOCK)],
        src[pl.ds(pl.multiple_of(at + BLOCK, BLOCK), HALF)],
        meta[LEFT + b],
        meta[RIGHT + b],
    )


def fill_first(pad, meta, src, low):
    fill(pad, low, src[0:BLOCK], src[BLOCK : BLOCK + HALF], meta[LEFT], meta[RIGHT])


def fill_last(pad, meta, src, high):
    rows = src.shape[0]
    last = rows // BLOCK - 1
    fill(
        pad,
        src[rows - BLOCK - HALF : rows - BLOCK],
        src[rows - BLOCK :],
        high,
        meta[LEFT + last],
        meta[RIGHT + last],
    )


def slabs(pad, lanes, first):
    for p in range(8):
        offsets = [o for o in range(first, first + TAPS) if o % 8 == p]
        count = BLOCK + 8 * (offsets[-1] // 8)
        yield pad[pl.ds(p, count), lanes].reshape(count // 8, 8, LANES), offsets


def depthwise(pad, taps, lanes, first, tap_of, block=BLOCK):
    count = block // 8 + 1
    padded = pad[:, lanes].reshape(pad.shape[0] // 8, 8, LANES)
    total = None
    for p in range(8):
        offsets = [o for o in range(first, first + TAPS) if o % 8 == p]
        part = None
        for o in offsets:
            i = tap_of(o)
            rows = count if p else count - 1
            term = padded[o // 8 : o // 8 + rows] * taps[i : i + 1, lanes][None]
            part = term if part is None else part + term
        part = part.reshape(-1, LANES)
        if p:
            part = pltpu.roll(part, part.shape[0] - p, 0)[:block]
        total = part if total is None else total + part
    return total


def lane_tiles(width):
    return lambda body: pl.loop(0, width // LANES)(
        lambda c: body(pl.ds(pl.multiple_of(c * LANES, LANES), LANES))
    )


def pad_by_step(inner, meta, src, low, high, pad, beyond):
    step = pl.program_id(0)
    if inner:
        b = step + 1
        fill_inner(pad, meta, b, src)
        return b
    rows = src.shape[0]

    @pl.when(step == 0)
    def _():
        fill_first(pad, meta, src, low[HALF:])
        beyond[: 2 * HALF] = low[...].astype(F32)
        beyond[2 * HALF :] = src[:HALF].astype(F32)

    @pl.when(step == 1)
    def _():
        fill_last(pad, meta, src, high[:HALF])
        beyond[:HALF] = src[rows - HALF :].astype(F32)
        beyond[HALF:] = high[...].astype(F32)

    return step * (rows // BLOCK - 1)


def activate(conv, gain, normed_ref, inverse_ref, slope_ref, swished_ref=None):
    width = conv.shape[1]
    mean, inverse = row_stats(lambda t: conv[:, t], width)
    inverse_ref[...] = inverse
    for t in tiles(width):
        normed = (conv[:, t] - mean) * inverse
        scaled = normed * gain[:, t]
        sig = jax.nn.sigmoid(scaled)
        swished = scaled * sig
        normed_ref[:, t] = normed.astype(BF16)
        slope_ref[:, t] = (sig + swished * (1.0 - sig)) * gain[:, t]
        if swished_ref is not None:
            swished_ref[:, t] = swished.astype(BF16)


def conv_kernel(inner, meta, *refs):
    if inner:
        src, taps, gain, *outs, pad, conv, beyond, far = refs
        low = high = None
    else:
        src, taps, gain, low, high, _, _, _, _, *outs, pad, conv, beyond, far = refs
    width = src.shape[1]
    b = pad_by_step(inner, meta, src, low, high, pad, beyond)
    valid = below(meta[COUNT + b], BLOCK)
    far_valid = below(jnp.where(pl.program_id(0) == 0, HALF, meta[NEXT]), HALF)

    @lane_tiles(width)
    def _(lanes):
        conv[:, lanes] = jnp.where(valid, depthwise(pad, taps, lanes, 0, lambda o: o), 0.0)
        if not inner:
            found = depthwise(beyond, taps, lanes, 0, lambda o: o, HALF)
            far[:, lanes] = jnp.where(far_valid, found, 0.0)

    activate(conv, gain, *outs[:4])
    if not inner:
        activate(far, gain, *outs[4:])


def split_call(kernel, inner, meta, operands, edges, held, outs, width, flops):
    rows = operands[0].shape[0]
    last = rows // BLOCK - 1

    def place(n, _):
        return (n + 1 if inner else n * last, 0)

    in_specs = []
    for a in operands:
        if a.shape[0] == rows and a is not operands[0]:
            in_specs.append(pl.BlockSpec((BLOCK, a.shape[1]), place))
        else:
            in_specs.append(whole(a.shape))
    args = list(operands)
    aliases = {}
    if not inner:
        args += map(in_hbm, edges)
        in_specs += [whole(e.shape) for e in edges]
        for n, h in enumerate(held):
            aliases[1 + len(args)] = n
            args.append(in_hbm(h) if outs[n][2] is pltpu.HBM else h)
            in_specs.append(pl.BlockSpec(memory_space=pl.ANY))
    return pl.pallas_call(
        functools.partial(kernel, inner),
        out_shape=[o[2](*o[:2]) for o in outs],
        grid_spec=pltpu.PrefetchScalarGridSpec(
            num_scalar_prefetch=1,
            grid=(2,),
            in_specs=in_specs,
            out_specs=[
                pl.BlockSpec((BLOCK, o[0][1]), place)
                if o[0][0] == rows
                else pl.BlockSpec((HALF, o[0][1]), lambda n, _: (n, 0))
                for o in outs
            ],
            scratch_shapes=[
                pltpu.VMEM((BLOCK + 2 * HALF, width), F32),
                pltpu.VMEM((BLOCK, width), F32),
                pltpu.VMEM((3 * HALF, width), F32),
                pltpu.VMEM((HALF, width), F32),
            ],
        ),
        input_output_aliases=aliases,
        compiler_params=params(16),
        cost_estimate=cost(),
        name=kernel.__name__ + ("_inner" if inner else "_edges"),
    )(meta, *args)


def conv_forward(inner, meta, glu, taps, gain, edges=(), held=()):
    rows, width = glu.shape
    outs = [
        ((rows, width), BF16, pltpu.HBM),
        ((rows, 1), F32, pltpu.HBM),
        ((rows, width), F32, pltpu.HBM),
        ((rows, width), BF16, jax.ShapeDtypeStruct),
    ]
    if not inner:
        outs += [((2 * HALF, o[0][1]), *o[1:]) for o in outs[:3]]
    return split_call(
        conv_kernel,
        inner,
        meta,
        (glu, taps, gain),
        edges,
        held,
        outs,
        width,
        4 * 10**9,
    )


def multiply_kernel(x_ref, w_ref, out_ref):
    out_ref[...] = jnp.dot(x_ref[...], w_ref[...], preferred_element_type=F32).astype(BF16)


def multiply(x, weight, tile=512):
    rows, depth = x.shape
    width = weight.shape[1]
    return pl.pallas_call(
        multiply_kernel,
        out_shape=jax.ShapeDtypeStruct((rows, width), BF16),
        grid=(width // tile,),
        in_specs=[whole((rows, depth)), pl.BlockSpec((depth, tile), lambda n: (0, n))],
        out_specs=pl.BlockSpec((rows, tile), lambda n: (0, n)),
        compiler_params=params(12),
        cost_estimate=cost(),
        name="multiply",
    )(x, in_hbm(weight))


def norm_back(load, normed_ref, inverse_ref, rows, width, first=None):
    normed = {t.start: normed_ref[rows, t].astype(F32) for t in tiles(width)}
    mean = row_total(load(t) for t in tiles(width)) * (1.0 / width)
    second = row_total(load(t) * normed[t.start] for t in tiles(width)) * (1.0 / width)
    if first is not None:
        rows = slice(first, first + rows.stop - rows.start)
    inverse = inverse_ref[rows]
    for t in tiles(width):
        yield t, (load(t) - mean - normed[t.start] * second) * inverse


def grad_conv_kernel(
    meta, grad_ref, w_ref, normed_ref, slope_ref, far_normed, far_slope, inverse_ref, far_inverse,
    out_ref, far_ref, incoming, normed,
):
    n = pl.program_id(0)
    rows, width = out_ref.shape
    tile = w_ref.shape[0]
    at = pl.ds(pl.multiple_of(n * tile, tile), tile)
    grad_s = lax.dot_general(
        grad_ref[...], w_ref[...], (((1,), (1,)), ((), ())), preferred_element_type=F32
    )
    incoming[:rows, at] = grad_s[:rows] * slope_ref[...]
    incoming[rows:, at] = grad_s[rows:] * far_slope[...]
    normed[:rows, at] = normed_ref[...]
    normed[rows:, at] = far_normed[...]

    def finish(ref, part, first, inverse, valid):
        count = part.stop - part.start
        for t, back in norm_back(
            lambda t: incoming[part, t], normed, inverse, part, width, first
        ):
            ref[first : first + count, t] = jnp.where(valid, back, 0.0).astype(BF16)

    @pl.when(n == pl.num_programs(0) - 1)
    def _():
        for b in range(rows // BLOCK):
            part = slice(b * BLOCK, (b + 1) * BLOCK)
            finish(out_ref, part, b * BLOCK, inverse_ref, below(meta[COUNT + b], BLOCK))
        part = slice(rows, rows + 2 * HALF)
        finish(far_ref, part, 0, far_inverse, below(HALF + meta[NEXT], 2 * HALF))


def grad_conv_call(meta, around, weight, normed, inverse, slope, far, tile=512):
    rows, width = normed.shape
    far_normed, far_inverse, far_slope = far
    column = pl.BlockSpec((rows, tile), lambda n, _: (0, n))
    beyond = pl.BlockSpec((2 * HALF, tile), lambda n, _: (0, n))
    return pl.pallas_call(
        grad_conv_kernel,
        out_shape=[pltpu.HBM((rows, width), BF16), pltpu.HBM((2 * HALF, width), BF16)],
        grid_spec=pltpu.PrefetchScalarGridSpec(
            num_scalar_prefetch=1,
            grid=(width // tile,),
            in_specs=[
                whole(around.shape),
                pl.BlockSpec((tile, width), lambda n, _: (n, 0)),
                column,
                column,
                beyond,
                beyond,
                whole(inverse.shape),
                whole(far_inverse.shape),
            ],
            out_specs=[whole((rows, width)), whole((2 * HALF, width))],
            scratch_shapes=[
                pltpu.VMEM((rows + 2 * HALF, width), F32),
                pltpu.VMEM((rows + 2 * HALF, width), BF16),
            ],
        ),
        compiler_params=params(28),
        cost_estimate=cost(),
        name="grad_conv",
    )(
        meta,
        around,
        in_hbm(weight),
        *map(in_hbm, (normed, slope, far_normed, far_slope, inverse, far_inverse)),
    )


def pad_by_block(meta, src, low, high, pad):
    b = pl.program_id(0)
    last = pl.num_programs(0) - 1

    @pl.when(b == 0)
    def _():
        fill_first(pad, meta, src, low())

    @pl.when(b == last)
    def _():
        fill_last(pad, meta, src, high())

    @pl.when((b > 0) & (b < last))
    def _():
        fill_inner(pad, meta, b, src)


def taps_kernel(scale, meta, src, grad_ref, low, high, out_ref, pad, total):
    b = pl.program_id(0)
    last = pl.num_programs(0) - 1
    width = src.shape[1]
    pad_by_block(meta, src, lambda: low[HALF:], lambda: high[:HALF], pad)

    @pl.when(b == 0)
    def _():
        total[...] = jnp.zeros_like(total)

    @lane_tiles(width)
    def _(lanes):
        grad = grad_ref[:, lanes].astype(F32).reshape(BLOCK // 8, 8, LANES)
        for slab, offsets in slabs(pad, lanes, 0):
            for o in offsets:
                total[o, :, lanes] += jnp.sum(
                    slab[o // 8 : o // 8 + BLOCK // 8] * grad, axis=0
                )

    @pl.when(b == last)
    def _():
        groups, few = out_ref.shape[0], out_ref.shape[1] // 2
        half = width // 2
        for g in range(groups):
            own = jnp.sum(total[g * few : (g + 1) * few], axis=1) * scale
            out_ref[g, :few] = own[:, :half]
            out_ref[g, few:] = own[:, half:]


def taps_gradient(meta, glu, grad_conv, edges, groups, scale):
    rows, width = glu.shape
    return pl.pallas_call(
        functools.partial(taps_kernel, scale),
        out_shape=jax.ShapeDtypeStruct((groups, 2 * TAPS // groups, width // 2), F32),
        grid_spec=pltpu.PrefetchScalarGridSpec(
            num_scalar_prefetch=1,
            grid=(rows // BLOCK,),
            in_specs=[
                whole(glu.shape),
                pl.BlockSpec((BLOCK, width), lambda n, _: (n, 0)),
                whole((2 * HALF, width)),
                whole((2 * HALF, width)),
            ],
            out_specs=whole((groups, 2 * TAPS // groups, width // 2)),
            scratch_shapes=[
                pltpu.VMEM((BLOCK + 2 * HALF, width), F32),
                pltpu.VMEM((TAPS, 8, width), F32),
            ],
        ),
        compiler_params=params(16),
        cost_estimate=cost(),
        name="taps_gradient",
    )(meta, glu, in_hbm(grad_conv), *map(in_hbm, edges))


def back_kernel(meta, src, taps, gate_ref, slope_ref, far, out_ref, pad):
    b = pl.program_id(0)
    width = src.shape[1]
    pad_by_block(meta, src, lambda: far[:HALF], lambda: far[HALF:], pad)
    valid = below(meta[COUNT + b], BLOCK)

    @pl.loop(0, width // LANES)
    def _(c):
        at = pl.multiple_of(c * LANES, LANES)
        lanes = pl.ds(at, LANES)
        grad = jnp.where(valid, depthwise(pad, taps, lanes, 1, lambda o: TAPS - o), 0.0)
        out_ref[:, lanes] = (grad * gate_ref[:, lanes]).astype(BF16)
        out_ref[:, pl.ds(pl.multiple_of(at + width, LANES), LANES)] = (
            grad * slope_ref[:, lanes]
        ).astype(BF16)


def conv_backward(meta, grad_conv, far, taps, gate, slope):
    rows, width = grad_conv.shape
    block = pl.BlockSpec((BLOCK, width), lambda n, _: (n, 0))
    return pl.pallas_call(
        back_kernel,
        out_shape=pltpu.HBM((rows, 2 * width), BF16),
        grid_spec=pltpu.PrefetchScalarGridSpec(
            num_scalar_prefetch=1,
            grid=(rows // BLOCK,),
            in_specs=[
                whole(grad_conv.shape),
                whole(taps.shape),
                block,
                block,
                whole(far.shape),
            ],
            out_specs=pl.BlockSpec((BLOCK, 2 * width), lambda n, _: (n, 0)),
            scratch_shapes=[pltpu.VMEM((BLOCK + 2 * HALF, width), F32)],
        ),
        compiler_params=params(16),
        cost_estimate=cost(),
        name="conv_backward",
    )(meta, in_hbm(grad_conv), taps, in_hbm(gate), in_hbm(slope), in_hbm(far))


def folded(values):
    return functools.reduce(
        lambda a, b: a + b, [values[:, t] for t in tiles(values.shape[1])]
    )


def input_kernel(
    gain_ref, grad_ref, w_ref, normed_ref, inverse_ref, out_ref, incoming, normed, first, second
):
    n = pl.program_id(0)
    rows, width = incoming.shape
    tile = w_ref.shape[0]
    at = pl.ds(pl.multiple_of(n * tile, tile), tile)

    @pl.when(n == 0)
    def _():
        first[...] = jnp.zeros_like(first)
        second[...] = jnp.zeros_like(second)

    g = gain_ref[:, at] * lax.dot_general(
        grad_ref[...], w_ref[...], (((1,), (1,)), ((), ())), preferred_element_type=F32
    )
    incoming[:, at] = g
    normed[:, at] = normed_ref[...]
    first[...] += folded(g)
    second[...] += folded(g * normed_ref[...].astype(F32))

    @pl.when(n == pl.num_programs(0) - 1)
    def _():
        for start in range(0, rows, BLOCK):
            part = slice(start, start + BLOCK)
            one = jnp.sum(first[part], axis=1, keepdims=True) * (1.0 / width)
            two = jnp.sum(second[part], axis=1, keepdims=True) * (1.0 / width)
            inverse = inverse_ref[part]
            for t in tiles(width):
                back = incoming[part, t] - one - normed[part, t].astype(F32) * two
                out_ref[part, t] = (back * inverse).astype(BF16)


def input_gradient(gain, grad_proj, weight, normed, inverse, tile=512):
    rows = grad_proj.shape[0]
    width = weight.shape[0]
    return pl.pallas_call(
        input_kernel,
        out_shape=jax.ShapeDtypeStruct((rows, width), BF16),
        grid=(width // tile,),
        in_specs=[
            whole((1, width)),
            whole(grad_proj.shape),
            pl.BlockSpec((tile, weight.shape[1]), lambda n: (n, 0)),
            pl.BlockSpec((rows, tile), lambda n: (0, n)),
            whole(inverse.shape),
        ],
        out_specs=whole((rows, width)),
        scratch_shapes=[
            pltpu.VMEM((rows, width), F32),
            pltpu.VMEM((rows, width), BF16),
            pltpu.VMEM((rows, LANES), F32),
            pltpu.VMEM((rows, LANES), F32),
        ],
        compiler_params=params(28),
        cost_estimate=cost(),
        name="input_gradient",
    )(gain, in_hbm(grad_proj), in_hbm(weight), in_hbm(normed), in_hbm(inverse))


def halves_of_neighbours(low, high):
    count = lax.axis_size("dp")
    forward = [(i, i + 1) for i in range(count - 1)]
    backward = [(i + 1, i) for i in range(count - 1)]
    return lax.ppermute(high, "dp", forward), lax.ppermute(low, "dp", backward)


def swap(values, axis, bits):
    return lax.ppermute(values, axis, [(i, i ^ bits) for i in range(lax.axis_size(axis))])


def sum_of_four(values, axis, low_bit):
    one, two = low_bit, 2 * low_bit
    first, second, third = (swap(values, axis, b) for b in (one, two, one + two))
    return (values + first) + (second + third)


def sum_of_chip(groups, core):
    groups = groups.reshape((groups.shape[0] // 2, 2) + groups.shape[1:])
    other = lax.dynamic_index_in_dim(groups, 1 - core, axis=1, keepdims=False)
    own = lax.dynamic_index_in_dim(groups, core, axis=1, keepdims=False)
    return own + swap(other, "fsdp", 1)


def sum_along_x(groups):
    mine = lax.axis_index("fsdp") // 2
    total = lax.dynamic_index_in_dim(groups, mine, keepdims=False)
    for bits in range(1, groups.shape[0]):
        theirs = lax.dynamic_index_in_dim(groups, mine ^ bits, keepdims=False)
        total = total + swap(theirs, "fsdp", 2 * bits)
    return total


def spread(values, axis):
    return lax.all_to_all(values, axis, split_axis=0, concat_axis=0, tiled=True)


def outer(left, right):
    return lax.dot_general(left, right, (((0,), (0,)), ((), ())), preferred_element_type=F32)


def half_of(values, which):
    half = values.shape[1] // 2
    return lax.dynamic_slice_in_dim(values, which * half, half, axis=1)


def half_for_other(left, right, core):
    return swap(outer(left, half_of(right, 1 - core)).astype(BF16), "fsdp", 1)


def with_own_half(left, right, core, arrived):
    return (outer(left, half_of(right, core)) + arrived.astype(F32)).astype(BF16)


def send_over_dp(both):
    count = lax.axis_size("dp")
    return spread(both.reshape((count, both.shape[0] // count) + both.shape[1:]), "dp")


def summed_over_dp(sent, scale):
    total = jnp.sum(sent.astype(F32), axis=0) * scale
    count = lax.axis_size("fsdp")
    return total.reshape((count, total.shape[0] // count) + total.shape[1:])


def last_exchange(taps_rows, pieces):
    taps_rows = jnp.broadcast_to(taps_rows[None], pieces.shape[:1] + taps_rows.shape)
    return spread(jnp.concatenate([taps_rows, pieces], axis=1), "fsdp")


def after_exchange(got, few):
    count, _, half = got.shape
    left = got[:, :few].reshape(count * few, half)
    right = got[:, few : 2 * few].reshape(count * few, half)
    pieces = got[:, 2 * few :]
    pieces = jnp.sum(pieces.reshape((count // 2, 2) + pieces.shape[1:]), axis=0)
    return (
        jnp.concatenate([left, right], axis=1),
        jnp.concatenate([pieces[0], pieces[1]], axis=1),
    )


def scalars(packing, counts, tails, place, blocks):
    mine = place * blocks + jnp.arange(blocks, dtype=jnp.int32)
    number = jnp.arange(counts.shape[0], dtype=jnp.int32)
    ends = jnp.sum(jnp.where(number[:, None] <= number[None, :], counts[:, None], 0), axis=0)
    opens = (ends - counts)[None, :] == mine[:, None]
    closes = (ends - 1)[None, :] == mine[:, None]
    left = 1 - jnp.sum(opens.astype(jnp.int32), axis=1)
    right = 1 - jnp.sum(closes.astype(jnp.int32), axis=1)
    valid = BLOCK + jnp.sum(jnp.where(closes, tails[None, :] - BLOCK, 0), axis=1)
    number = jnp.arange(packing.shape[0], dtype=jnp.int32)
    slot = jnp.sum(
        jnp.where(packing[None, :] == mine[:, None], number[None, :] % blocks, 0), axis=1
    )
    closes = ends - 1 == (place + 1) * blocks
    after = BLOCK + jnp.sum(jnp.where(closes, tails - BLOCK, 0), keepdims=True)
    return jnp.concatenate([left, right, valid, slot, after]).astype(jnp.int32)


def target_order(packing, place, blocks):
    count = packing.shape[0] // blocks
    color = place // blocks
    number = jnp.arange(packing.shape[0], dtype=jnp.int32)
    chosen = (number % blocks == color)[None, :]
    goes = (packing // blocks)[None, :] == jnp.arange(count, dtype=jnp.int32)[:, None]
    return jnp.sum(jnp.where(chosen & goes, (number // blocks)[None, :], 0), axis=1)


def local(
    inputs,
    norm_gain,
    weight_in,
    kernel,
    conv_gain,
    weight_out,
    out_grad,
    pack_dest,
    utt_blocks,
    tail_frames,
):
    dp_count = lax.axis_size("dp")
    place = lax.axis_index("dp")
    core = lax.axis_index("fsdp") % 2
    rows, width = inputs.shape[2:]
    blocks = rows // BLOCK
    scale = 1.0 / math.sqrt(rows * lax.axis_size(("dp", "fsdp")))
    full_in = lax.all_gather(weight_in, "fsdp", axis=0, tiled=True)
    full_out = lax.all_gather(weight_out, "fsdp", axis=0, tiled=True)
    meta = scalars(pack_dest[0], utt_blocks[0], tail_frames[0], place, blocks)
    order = target_order(pack_dest[0], place, blocks)
    gain_in = norm_gain.reshape(1, width)
    gain_conv = conv_gain.reshape(1, width)

    quarters = spread(inputs.reshape(dp_count, rows // dp_count, width), "dp")
    upstream = out_grad[0, 0]
    beyond = halves_of_neighbours(upstream[:HALF], upstream[rows - HALF :])
    order, beyond = lax.optimization_barrier((order, beyond))
    around = jnp.concatenate([upstream, *beyond])
    meta, around = lax.optimization_barrier((meta, around))
    arrived = spread(reorder(order, quarters), "dp")

    normed_in, inverse_in, gate, gate_slope, glu, low, high = project(
        meta, arrived, gain_in, full_in
    )
    glu_edges = halves_of_neighbours(low, high)
    held = conv_forward(True, meta, glu, kernel, gain_conv)
    normed, inverse, slope, swished, *far = conv_forward(
        False, meta, glu, kernel, gain_conv, glu_edges, held
    )

    arrived = half_for_other(swished, upstream, core)
    grad_conv, far = grad_conv_call(meta, around, full_out, normed, inverse, slope, far)
    arrived, grad_conv = lax.optimization_barrier((arrived, grad_conv))
    both = with_own_half(swished, upstream, core, arrived)
    sent = send_over_dp(both)
    fsdp_count = lax.axis_size("fsdp")
    taps_rows = taps_gradient(meta, glu, grad_conv, glu_edges, fsdp_count, scale)
    taps_rows = sum_of_chip(taps_rows, core)
    taps_rows, grad_conv = lax.optimization_barrier((taps_rows, grad_conv))
    grad_proj = conv_backward(meta, grad_conv, far, kernel, gate, gate_slope)
    taps_rows = sum_along_x(taps_rows)
    taps_rows, grad_proj, swished = lax.optimization_barrier((taps_rows, grad_proj, swished))
    module_out = multiply(swished, full_out)
    taps_rows, sent, module_out = lax.optimization_barrier((taps_rows, sent, module_out))
    pieces = summed_over_dp(sent, scale)
    taps_rows = sum_of_four(taps_rows, "dp", 1)
    taps_rows = sum_of_four(taps_rows, "dp", 4)
    taps_rows, pieces, grad_proj = lax.optimization_barrier((taps_rows, pieces, grad_proj))
    got = last_exchange(taps_rows, pieces)
    kernel_grad, weight_out_grad = after_exchange(got, TAPS // fsdp_count)
    input_grad = input_gradient(gain_in, grad_proj, full_in, normed_in, inverse_in)
    return (
        module_out.reshape(1, 1, rows, width),
        input_grad.reshape(1, 1, rows, width),
        weight_out_grad,
        kernel_grad,
    )


def solution(mesh):
    in_specs = (
        P("dp", "fsdp", None, None),
        P(),
        P("fsdp", None),
        P(),
        P(),
        P("fsdp", None),
        P("dp", "fsdp", None, None),
        P("fsdp", None),
        P("fsdp", None),
        P("fsdp", None),
    )
    out_specs = (
        P("dp", "fsdp", None, None),
        P("dp", "fsdp", None, None),
        P(("dp", "fsdp"), None),
        P(),
    )
    return jax.shard_map(local, mesh=mesh, in_specs=in_specs, out_specs=out_specs, check_vma=False)
```
